256 devices in a mesh: grp: 32 (over x_hi, z, core), ep: 8 (over y, x_lo).
Axes of the slice: x: 4 (x_hi: 2, x_lo: 2; x = x_hi * 2 + x_lo), y: 4, z: 8, core: 2. Of those that a mesh axis runs over, the one named last changes fastest.
Arguments:
- kv_pages: bfloat16 [8192, 64, 576], P(('grp', 'ep')), may hold values from -6 to 6
- page_dest: int32 [8, 1024, 1], P('ep'), may hold values from 0 to 31; in each aligned block of 32 rows (0 to 31, 32 to 63, ..., all dimensions but the last counted through in order) at most 2 rows name the same one
- page_req: int32 [8, 1024], P('ep'), may hold values from 0 to 1
- page_fill: int32 [8, 1024], P('ep'), may hold values from 1 to 64
- queries: bfloat16 [512, 128, 576], P(('grp', 'ep')), may hold values from -250 to 250
- new_latent: bfloat16 [512, 576], P(('grp', 'ep')), may hold values from -6 to 6
- moe_in: bfloat16 [256, 7168], P(('grp', 'ep')), may hold values from -6 to 6
- route_ids: int32 [256, 8], P(('grp', 'ep')), may hold values from 0 to 15, all different within a row
- route_w: float32 [256, 8], P(('grp', 'ep')), may hold values from 0.1 to 0.5
- w_gate: bfloat16 [16, 2048, 7168], P('ep', 'grp'), may hold values from -0.0625 to 0.0625
- w_up: bfloat16 [16, 2048, 7168], P('ep', 'grp'), may hold values from -0.0625 to 0.0625
- w_down: bfloat16 [16, 2048, 7168], P('ep', 'grp'), may hold values from -0.125 to 0.125
Outputs:
- attn_latent: bfloat16 [512, 128, 512], P(('grp', 'ep'))
- moe_out: bfloat16 [256, 7168], P(('grp', 'ep'))
The draws below stay inside these ranges and needn't reach their ends.
Inputs may be any that keep to these rules, and one draw needn't show every extreme that they name: `page_dest`: at most 2 pages of one device go to one decode group index; some device sends exactly 2 to one.
All inputs are finite; a program needn't handle non-finite values.
Results may differ from the reference program's by a relative error of at most 0.006.
Values may be sent and summed in bfloat16 or wider, within the bound.
A program may use at most 128 MiB of HBM per device.

```python
import math
import jax
import jax.numpy as jnp
import numpy as np
from jax import lax

D = 7168
FE = 2048
H = 128
KV_L = 512
KW = 576
TOPK = 8
EXPERTS = 16
PAGE = 64
PAGES_DEV = 32
CAP = 2
PAGES = 8192
REQ_DEV = 2
REQS = 512
TOKENS = 256
N_GRP = 32
N_EP = 8


def draw_queries(key, part):
    key = jax.random.fold_in(key, 11)
    base = jnp.clip(jax.random.normal(key, (REQS, H, KW), jnp.float32), -6.0, 6.0)
    return base.astype(jnp.bfloat16)


def set_ends(entries, rng, smallest, high):
    extent = entries.shape
    index_at = [jax.random.randint(jax.random.fold_in(rng, axis), (), 0, extent[axis]) for axis in range(len(extent))]
    entries = entries.at[tuple(index_at)].set(smallest)
    longest = extent.index(max(extent))
    index_at[longest] = (index_at[longest] + 1) % extent[longest]
    return entries.at[tuple(index_at)].set(high)


def block_scale(key, extent, shards, least, top_value):
    level = 1.0
    for axis_at, shards_of in shards:
        steps = jax.random.uniform(jax.random.fold_in(jax.random.fold_in(key, 6), axis_at), (shards_of,), jnp.float32, least / len(shards), top_value / len(shards))
        level = level * jnp.repeat(jnp.exp(steps), extent[axis_at] // shards_of).reshape((-1,) + (1,) * (len(extent) - 1 - axis_at))
    return level


def distinct(key, rows, amount, top, lift):
    sequence = jax.random.permutation(jax.random.fold_in(key, 1), amount)
    pull = sequence
    for power in range(3):
        pull = pull * pull // amount
    pull = pull * lift // amount
    tickets = jax.random.randint(jax.random.fold_in(key, 2), (rows, amount), 0, 4096) + pull
    fixed_rows = jax.random.permutation(jax.random.fold_in(key, 3), rows)[jnp.arange(amount) % rows]
    tickets = jnp.where(jnp.arange(rows)[:, None] == fixed_rows[None, :], 1 << 14, tickets)
    merit = tickets * amount + jnp.arange(amount)
    return lax.top_k(merit.astype(jnp.int32), top)[1].astype(jnp.int32)


def assign_block(rng, own, number, rows, count, top, most, lean):
    order = jax.random.permutation(rng, count)
    crowded, usual = shares(count, rows * top, most, lean, True), shares(count, rows * top, most, lean, False)
    places = jnp.arange(count)

    def named(sizes, rotation):
        used = int((sizes > 0).sum())
        fixed = max(1, used // 4)
        moved = fixed + (places - fixed + rotation * (used - fixed)) % max(1, count - fixed)
        return jnp.zeros((count,), jnp.int32).at[order[jnp.where(places < fixed, places, moved)]].set(jnp.asarray(sizes, jnp.int32))

    sizes = jnp.where(number % 4 == 0, named(crowded, number // 4), named(usual, number - number // 4 - 1))
    mixed = jax.random.permutation(jax.random.fold_in(own, 3), count)
    donor, sink = mixed[0:count // 2 * 2:2], mixed[1:count // 2 * 2:2]
    margin = jnp.minimum(sizes[donor] - 1, most - sizes[sink]) // 2
    margin = jnp.where((donor == order[0]) | (sink == order[0]) | (sizes[sink] == 0), 0, jnp.maximum(margin, 0))
    moved = jax.random.randint(jax.random.fold_in(own, 4), (count // 2,), 0, 1 << 20) % (margin + 1)
    sizes = sizes.at[donor].add(-moved).at[sink].add(moved)
    members = jnp.searchsorted(jnp.cumsum(sizes), jnp.arange(rows * top), side="right").astype(jnp.int32)
    listing = members.reshape(top, rows).T
    listing = listing[jax.random.permutation(jax.random.fold_in(own, 1), rows)]
    rotation = jax.random.randint(jax.random.fold_in(own, 2), (rows, 1), 0, top)
    return jnp.take_along_axis(listing, (jnp.arange(top)[None, :] + rotation) % top, axis=1)


def shares(count, total, reach, skew, full):
    loads = [(1 << 20) // math.isqrt(standing ** skew) + 1 for standing in range(1, count + 1)]
    largest = reach if full else min(reach, max(-(-total // count), total * loads[0] // sum(loads)))
    least = 1 if total - largest >= count - 1 else 0
    holding, surplus = [largest] + [least] * (count - 1), total - largest - least * (count - 1)
    while surplus > 0:
        free = [i for i in range(1, count) if holding[i] < largest] or [i for i in range(1, count) if holding[i] < reach]
        whole, remaining = sum([loads[i] for i in free]), surplus
        for i in free:
            addition = min(reach - holding[i], max(1, remaining * loads[i] // whole), surplus)
            holding[i] = holding[i] + addition
            surplus = surplus - addition
    return np.array(holding)


def normal_values(rng, dims, deviation, limit, split=(), kind=jnp.bfloat16):
    values = jax.random.normal(rng, dims, jnp.float32) * deviation
    if len(split) > 0:
        values = block_scale(rng, dims, split, -0.22, 0.18) * values
    return jnp.clip(values, min=-limit, max=limit).astype(kind)


def setup_inputs(seed: int = 0) -> dict:
    streams_of = jax.random.split(jax.random.key(seed), 13)
    kv_pages = normal_values(streams_of[0], (PAGES, PAGE, KW), 1.0, 6.0, ((0, 256),))
    page_dest_keys = jax.random.split(jax.random.fold_in(streams_of[1], 1), N_EP * (N_GRP * PAGES_DEV) // PAGES_DEV)
    page_dest_turns = jax.random.permutation(jax.random.fold_in(streams_of[1], 3), N_EP * (N_GRP * PAGES_DEV) // PAGES_DEV)
    page_dest = jax.vmap(lambda own, number: assign_block(jax.random.fold_in(streams_of[1], 2), own, number, PAGES_DEV, N_GRP, 1, CAP, 2))(page_dest_keys, page_dest_turns).reshape((N_EP, N_GRP * PAGES_DEV, 1))
    page_req = set_ends(jax.random.randint(streams_of[2], (N_EP, N_GRP * PAGES_DEV), 0, REQ_DEV), jax.random.fold_in(streams_of[2], 1), 0, REQ_DEV - 1).astype(jnp.int32)
    page_fill = set_ends(jax.random.randint(streams_of[3], (N_EP, N_GRP * PAGES_DEV), 1, PAGE + 1), jax.random.fold_in(streams_of[3], 1), 1, PAGE).astype(jnp.int32)
    queries = draw_queries(jax.random.fold_in(streams_of[12], 71), 0)
    new_latent = normal_values(streams_of[5], (REQS, KW), 1.0, 6.0, ((0, 256),))
    moe_in = normal_values(streams_of[6], (TOKENS, D), 1.0, 6.0, ((0, 256),))
    route_ids = distinct(streams_of[7], TOKENS, EXPERTS, TOPK, 8192)
    route_w = jnp.clip(0.1 + 0.4 * jax.random.uniform(streams_of[8], (TOKENS, TOPK), jnp.float32) ** block_scale(streams_of[8], (TOKENS, TOPK), ((0, 256),), -0.2, 0.2), 0.1, 0.5)
    w_gate = normal_values(streams_of[9], (EXPERTS, FE, D), D ** -0.5, 0.0625, ((0, 8), (1, 32)))
    w_up = normal_values(streams_of[10], (EXPERTS, FE, D), D ** -0.5, 0.0625, ((0, 8), (1, 32)))
    w_down = normal_values(streams_of[11], (EXPERTS, FE, D), FE ** -0.5, 0.125, ((0, 8), (1, 32)))
    return dict(kv_pages=kv_pages, page_dest=page_dest, page_req=page_req, page_fill=page_fill, queries=queries, new_latent=new_latent, moe_in=moe_in, route_ids=route_ids, route_w=route_w, w_gate=w_gate, w_up=w_up, w_down=w_down)


SCALE = 192.0 ** -0.5


def page_ranks(dest, n_grp):
    onehot = (dest[:, :, None] == jnp.arange(n_grp, dtype=jnp.int32)[None, None, :]).astype(jnp.int32)
    before = jnp.cumsum(onehot, axis=1) - onehot
    return jnp.sum(before * onehot, axis=2)


def slot_select(dest, ranks, target, cap):
    slots = jnp.arange(cap, dtype=jnp.int32)
    hit = (dest == target)[:, :, None] & (ranks[:, :, None] == slots[None, None, :])
    return hit.astype(jnp.int32)


def attend(rows, own_key, keys, slot_req, slot_fill):
    count = rows.shape[0]
    flat = keys.reshape(-1, keys.shape[-1]).astype(jnp.float32)
    query = rows.astype(jnp.float32)
    own = own_key.astype(jnp.float32)
    scores = jnp.einsum("rhc,kc->rhk", query, flat) * SCALE
    own_score = jnp.einsum("rhc,rc->rh", query, own) * SCALE
    position = jnp.arange(keys.shape[1], dtype=jnp.int32)
    live = position[None, :] < slot_fill[:, None]
    mine = slot_req[None, :, None] == jnp.arange(count, dtype=jnp.int32)[:, None, None]
    mask = (mine & live[None, :, :]).reshape(count, 1, -1)
    peak = jnp.maximum(jnp.max(jnp.where(mask, scores, -jnp.inf), axis=2), own_score)
    weights = jnp.where(mask, jnp.exp(scores - peak[:, :, None]), 0.0)
    own_weight = jnp.exp(own_score - peak)
    total = jnp.sum(weights, axis=2) + own_weight
    weights_b = weights.astype(jnp.bfloat16).astype(jnp.float32)
    own_b = own_weight.astype(jnp.bfloat16).astype(jnp.float32)
    summed = jnp.einsum("rhk,kc->rhc", weights_b, flat[:, :KV_L])
    summed = summed + own_b[:, :, None] * own[:, None, :KV_L]
    return (summed / total[:, :, None]).astype(jnp.bfloat16)


def reference(kv_pages, page_dest, page_req, page_fill, queries, new_latent, moe_in, route_ids, route_w, w_gate, w_up, w_down):
    grid = kv_pages.reshape(N_GRP, N_EP, PAGES_DEV, PAGE, KW)
    counting = jnp.arange(PAGES_DEV, dtype=jnp.int32)

    def one_device(index):
        target = index // N_EP
        column = index % N_EP
        dest = lax.dynamic_index_in_dim(page_dest, column, 0, False)[:, 0].reshape(N_GRP, PAGES_DEV)
        req_tab = lax.dynamic_index_in_dim(page_req, column, 0, False).reshape(N_GRP, PAGES_DEV)
        fill_tab = lax.dynamic_index_in_dim(page_fill, column, 0, False).reshape(N_GRP, PAGES_DEV)
        ranks = page_ranks(dest, N_GRP)
        select = slot_select(dest, ranks, target, CAP)
        pick = jnp.sum(select * counting[None, :, None], axis=1).astype(jnp.int32)
        used = jnp.sum(select, axis=1)
        sources = jnp.broadcast_to(jnp.arange(N_GRP, dtype=jnp.int32)[:, None], pick.shape)
        columns = jnp.zeros(pick.shape, jnp.int32) + column
        keys = grid[sources, columns, pick] * used[:, :, None, None].astype(grid.dtype)
        slot_req = jnp.sum(select * req_tab[:, :, None], axis=1).reshape(-1)
        slot_fill = jnp.sum(select * fill_tab[:, :, None], axis=1).reshape(-1)
        rows = lax.dynamic_slice_in_dim(queries, (index * REQ_DEV).astype(jnp.int32), REQ_DEV, 0)
        own = lax.dynamic_slice_in_dim(new_latent, (index * REQ_DEV).astype(jnp.int32), REQ_DEV, 0)
        return attend(rows, own, keys.reshape(-1, PAGE, KW), slot_req, slot_fill)

    attn_latent = lax.map(one_device, jnp.arange(N_GRP * N_EP, dtype=jnp.int32)).reshape(REQS, H, KV_L)

    chosen = (route_ids[:, :, None] == jnp.arange(EXPERTS, dtype=jnp.int32)[None, None, :]).astype(jnp.float32)
    gates = jnp.sum(chosen * route_w[:, :, None], axis=1).astype(jnp.bfloat16)

    def one_expert(total, parts):
        gate_rows, up_rows, down_rows, gate_col = parts
        first = jnp.dot(moe_in, gate_rows.T, preferred_element_type=jnp.float32)
        second = jnp.dot(moe_in, up_rows.T, preferred_element_type=jnp.float32)
        hidden = (jax.nn.silu(first) * second).astype(jnp.bfloat16)
        return total + gate_col[:, None].astype(jnp.float32) * jnp.dot(hidden, down_rows, preferred_element_type=jnp.float32), None

    total, _ = lax.scan(one_expert, jnp.zeros((TOKENS, D), jnp.float32), (w_gate, w_up, w_down, gates.T))
    return attn_latent, total.astype(jnp.bfloat16)
```

```python
import functools

import jax
import jax.numpy as jnp
from jax import lax
from jax.experimental import pallas as pl
from jax.experimental.pallas import tpu as pltpu
from jax.sharding import PartitionSpec as P

MESH = pl.DeviceIdType.MESH
EXPERTS = 16
HALF = 3584
GW = HALF + 128
BF = jnp.bfloat16
F32 = jnp.float32


def coords():
    g = lax.axis_index("grp")
    e = lax.axis_index("ep")
    return (g // 16) * 2 + e % 2, e // 2, (g // 2) % 8, g % 2


def device(x, y, z, c):
    x, y, z, c = (x + 4) % 4, (y + 4) % 4, (z + 8) % 8, (c + 2) % 2
    return ((x // 2) * 16 + z * 2 + c, y * 2 + x % 2)


def ring_member(x, y, m):
    m = (m + 16) % 16
    return device(x, y, m // 2, m % 2)


def barrier(partners):
    sem = pltpu.get_barrier_semaphore()
    for p in partners:
        pl.semaphore_signal(sem, 1, device_id=p, device_id_type=MESH)
    pl.semaphore_wait(sem, len(partners))


def dot_t(a, b):
    return lax.dot_general(a, b, (((1,), (1,)), ((), ())), preferred_element_type=F32)


def moe_steps(r):
    x, y, z, c = coords()
    m = z * 2 + c
    mate = device(x, y, z, 1 - c)

    def push(src, dst, ss, rs, dev):
        cp = pltpu.make_async_remote_copy(src, dst, ss, rs, device_id=dev, device_id_type=MESH)
        cp.start()
        return cp

    loads = [
        pltpu.make_async_copy(r["wg"], r["w1"].at[pl.ds(0, 128)], r["lsem"].at[0]),
        pltpu.make_async_copy(r["wu"], r["w1"].at[pl.ds(128, 128)], r["lsem"].at[1]),
        pltpu.make_async_copy(r["wd"], r["w2"], r["lsem"].at[2]),
    ]
    tok, ra = r["tok"], r["ra"]
    cps = []
    for k in range(1, 16):
        mm = (m + k) % 16
        cps.append(push(tok.at[mm % 2], ra.at[m], r["sa"].at[0, k], r["sa"].at[1, k], ring_member(x, y, mm)))
    for cp in loads:
        cp.start()
    ra[m] = tok[c]
    yield
    for cp in cps:
        cp.wait()
    rows = lax.broadcasted_iota(jnp.int32, (464, 512), 0)
    cols = lax.broadcasted_iota(jnp.int32, (464, 512), 1)
    pick = jnp.where(cols == (rows % 16) * 32 + rows // 16, 1.0, 0.0).astype(BF)
    got = jnp.dot(pick, ra[...].reshape(512, 128), preferred_element_type=F32).astype(BF)
    xb = r["xb"]
    mine = y * 4 + x
    for j in range(29):
        xb[c, mine, :, j * 128 : (j + 1) * 128] = got[j * 16 : (j + 1) * 16]
    cps = []
    for i, k in enumerate((2, 1, 3)):
        cps.append(push(xb.at[c, mine], xb.at[c, mine], r["sb"].at[0, i], r["sb"].at[1, i], device(x + k, y, z, c)))
    yield
    for cp in cps:
        cp.wait()
    own = xb.at[c, pl.ds(y * 4, 4)]
    cps = []
    for i, k in enumerate((2, 1, 3)):
        cps.append(push(own, own, r["sc"].at[0, i], r["sc"].at[1, i], device(x, y + k, z, c)))
    dcps = [push(own, own, r["sd"].at[0, 3], r["sd"].at[1, 3], mate)]
    yield
    for i, k in ((1, 1), (2, 3), (0, 2)):
        cps[i].wait()
        blk = xb.at[c, pl.ds(((y - k + 4) % 4) * 4, 4)]
        dcps.append(push(blk, blk, r["sd"].at[0, i], r["sd"].at[1, i], mate))
        yield
    for cp in dcps:
        cp.wait()
    for cp in loads:
        cp.wait()
    w1, w2, acc = r["w1"], r["w2"], r["acc"]
    acc[...] = jnp.zeros_like(acc)
    for h in range(2):

        def step(k, carry, h=h):
            at = pl.multiple_of(k * 512, 512)
            a = xb[h, :, :, pl.ds(at, 512)].reshape(256, 512)
            b = w1[:, pl.ds(pl.multiple_of(h * HALF + at, 128), 512)]
            acc[...] += dot_t(a, b)
            return carry

        lax.fori_loop(0, 7, step, 0)
    first, second = acc[:, :128], acc[:, 128:]
    hidden = ((first / (1.0 + jnp.exp(-first))) * second).astype(BF).astype(F32)
    gates = xb[0, :, :, HALF : HALF + 128].reshape(256, 128).astype(F32)
    col = lax.axis_index("ep")
    lane = lax.broadcasted_iota(jnp.int32, (256, 128), 1)
    g0 = jnp.sum(jnp.where(lane == col * 2, gates, 0.0), axis=1, keepdims=True)
    g1 = jnp.sum(jnp.where(lane == col * 2 + 1, gates, 0.0), axis=1, keepdims=True)
    scaled = hidden * jnp.where(lane < 64, g0, g1)
    hi = scaled.astype(BF)
    lo = (scaled - hi.astype(F32)).astype(BF)
    ybf, yown, rc = r["ybf"], r["yown"], r["rc"]
    hl = jnp.concatenate([hi, lo], axis=1)

    def second_product(h, store):
        def step(k, carry):
            at = pl.multiple_of(k * 512, 512)
            w = w2[:, pl.ds(pl.multiple_of(h * HALF + at, 128), 512)]
            out = jnp.dot(hl, jnp.concatenate([w, w], axis=0), preferred_element_type=F32)
            store(at, out.reshape(16, 16, 512))
            return carry

        lax.fori_loop(0, 7, step, 0)

    def to_mate(at, v):
        ybf[:, :, pl.ds(at, 512)] = v.astype(BF)

    def to_own(at, v):
        yown[:, :, pl.ds(at, 512)] = v

    second_product(1 - c, to_mate)
    cps = []
    for k in range(4):
        blk = pl.ds(((y + k) % 4) * 4, 4)
        cps.append(push(ybf.at[blk], rc.at[blk], r["se"].at[0, k], r["se"].at[1, k], mate))
    second_product(c, to_own)
    yield
    s2, r2, yacc = r["s2"], r["r2"], r["yacc"]
    ycps = [None] * 3
    for k in (2, 1, 3, 0):
        blk = pl.ds(((y + k) % 4) * 4, 4)
        cps[k].wait()

        def step(q, carry, k=k, blk=blk):
            at = pl.multiple_of(q * 512, 512)
            v = yown[blk, :, pl.ds(at, 512)] + rc[blk, :, pl.ds(at, 512)].astype(F32)
            if k == 0:
                yacc[:, :, pl.ds(at, 512)] = v
            else:
                s2[k - 1, :, :, pl.ds(at, 512)] = v.astype(BF)
            return carry

        lax.fori_loop(0, 7, step, 0)
        if k:
            ycps[k - 1] = push(s2.at[k - 1], r2.at[k - 1], r["sf"].at[0, k], r["sf"].at[1, k], device(x, y + k, z, c))
    yield
    for cp in ycps:
        cp.wait()
    s3, r3, zacc = r["s3"], r["r3"], r["zacc"]
    xcps = [None] * 3
    for k in (2, 1, 3, 0):
        b = (x + k) % 4
        v = yacc[b]
        for i in range(3):
            v = v + r2[i, b].astype(F32)
        if k == 0:
            zacc[...] = v
        else:
            s3[k - 1] = v.astype(BF)
            xcps[k - 1] = push(s3.at[k - 1], r3.at[k - 1], r["sg"].at[0, k], r["sg"].at[1, k], device(x + k, y, z, c))
    yield
    for cp in xcps:
        cp.wait()
    v = zacc[...]
    for i in range(3):
        v = v + r3[i].astype(F32)
    vb = v.astype(BF)
    stack = jnp.concatenate([vb[:, j * 128 : (j + 1) * 128] for j in range(28)], axis=0)
    rows = lax.broadcasted_iota(jnp.int32, (512, 448), 0)
    cols = lax.broadcasted_iota(jnp.int32, (512, 448), 1)
    pick = jnp.where(cols == (rows % 32) * 16 + rows // 32, 1.0, 0.0).astype(BF)
    t4, r4 = r["t4"], r["r4"]
    t4[...] = jnp.dot(pick, stack, preferred_element_type=F32).astype(BF).reshape(16, 32, 128)
    cps = []
    for k in range(1, 16):
        mm = (m + k) % 16
        cps.append(push(t4.at[mm], r4.at[m], r["sh"].at[0, k], r["sh"].at[1, k], ring_member(x, y, mm)))
    r4[m] = t4[m]
    yield
    for cp in cps:
        cp.wait()
    for h in range(2):
        tot = r4[h].astype(F32)
        for i in range(1, 8):
            tot = tot + r4[2 * i + h].astype(F32)
        r["mo"][h] = tot.astype(BF)


MOE_SCRATCH = dict(
    w1=pltpu.VMEM((256, 2 * HALF), BF),
    w2=pltpu.VMEM((128, 2 * HALF), BF),
    ra=pltpu.VMEM((16, 32, 128), BF),
    xb=pltpu.VMEM((2, 16, 16, GW), BF),
    acc=pltpu.VMEM((256, 256), F32),
    ybf=pltpu.VMEM((16, 16, HALF), BF),
    yown=pltpu.VMEM((16, 16, HALF), F32),
    rc=pltpu.VMEM((16, 16, HALF), BF),
    s2=pltpu.VMEM((3, 4, 16, HALF), BF),
    r2=pltpu.VMEM((3, 4, 16, HALF), BF),
    yacc=pltpu.VMEM((4, 16, HALF), F32),
    s3=pltpu.VMEM((3, 16, HALF), BF),
    r3=pltpu.VMEM((3, 16, HALF), BF),
    zacc=pltpu.VMEM((16, HALF), F32),
    t4=pltpu.VMEM((16, 32, 128), BF),
    r4=pltpu.VMEM((16, 32, 128), BF),
    lsem=pltpu.SemaphoreType.DMA((3,)),
    sa=pltpu.SemaphoreType.DMA((2, 16)),
    sb=pltpu.SemaphoreType.DMA((2, 3)),
    sc=pltpu.SemaphoreType.DMA((2, 3)),
    sd=pltpu.SemaphoreType.DMA((2, 4)),
    se=pltpu.SemaphoreType.DMA((2, 4)),
    sf=pltpu.SemaphoreType.DMA((2, 4)),
    sg=pltpu.SemaphoreType.DMA((2, 4)),
    sh=pltpu.SemaphoreType.DMA((2, 16)),
)


def moe_partners():
    x, y, z, c = coords()
    m = z * 2 + c
    out = [ring_member(x, y, m + k) for k in range(1, 16)]
    out += [device(x + k, y, z, c) for k in (1, 2, 3)]
    out += [device(x, y + k, z, c) for k in (1, 2, 3)]
    return out


def moe_kernel(tok, wg, wu, wd, mo, *scratch):
    r = dict(zip(MOE_SCRATCH, scratch), tok=tok, wg=wg, wu=wu, wd=wd, mo=mo)
    barrier(moe_partners())
    for _ in moe_steps(r):
        pass


def moe_call(moe_in, route_ids, route_w, w_gate, w_up, w_down):
    chosen = (route_ids[:, :, None] == jnp.arange(EXPERTS, dtype=jnp.int32)[None, None, :]).astype(F32)
    gates = jnp.sum(chosen * route_w[:, :, None], axis=1).astype(BF)
    gate_row = jnp.pad(gates, ((0, 0), (0, 112)))
    tok = jnp.concatenate(
        [
            moe_in.reshape(2, 28, 128),
            jnp.broadcast_to(gate_row[None], (2, 1, 128)),
            jnp.zeros((2, 3, 128), BF),
        ],
        axis=1,
    )
    vm = pl.BlockSpec(memory_space=pltpu.VMEM)
    hb = pl.BlockSpec(memory_space=pl.ANY)
    out = pl.pallas_call(
        moe_kernel,
        name="experts",
        out_shape=jax.ShapeDtypeStruct((2, 32, 128), BF),
        in_specs=[vm, hb, hb, hb],
        out_specs=vm,
        scratch_shapes=list(MOE_SCRATCH.values()),
        compiler_params=pltpu.CompilerParams(collective_id=0, has_side_effects=True, vmem_limit_bytes=56 * 2**20),
    )(tok, w_gate.reshape(128, -1), w_up.reshape(128, -1), w_down.reshape(128, -1))
    return out[:, :28].reshape(1, 2 * HALF)


KV_L = 512


SCALE = 192.0 ** (-0.5)


def page_ranks(dest, n_grp):
    onehot = (dest[:, :, None] == jnp.arange(n_grp, dtype=jnp.int32)[None, None, :]).astype(
        jnp.int32
    )
    before = jnp.cumsum(onehot, axis=1) - onehot
    return jnp.sum(before * onehot, axis=2)


def attend(rows, own_key, keys, slot_req, slot_fill, latent_width):
    count = rows.shape[0]
    flat = keys.reshape(-1, keys.shape[-1])
    scores = jnp.einsum("rhc,kc->rhk", rows, flat, preferred_element_type=jnp.float32) * SCALE
    own_score = jnp.einsum("rhc,rc->rh", rows, own_key, preferred_element_type=jnp.float32) * SCALE
    position = jnp.arange(keys.shape[1], dtype=jnp.int32)
    live = position[None, :] < slot_fill[:, None]
    mine = slot_req[None, :, None] == jnp.arange(count, dtype=jnp.int32)[:, None, None]
    mask = (mine & live[None, :, :]).reshape(count, 1, -1)
    peak = jnp.maximum(jnp.max(jnp.where(mask, scores, -jnp.inf), axis=2), own_score)
    weights = jnp.where(mask, jnp.exp(scores - peak[:, :, None]), 0.0)
    own_weight = jnp.exp(own_score - peak)
    total = jnp.sum(weights, axis=2) + own_weight
    summed = jnp.einsum(
        "rhk,kc->rhc",
        weights.astype(jnp.bfloat16),
        flat[:, :latent_width],
        preferred_element_type=jnp.float32,
    )
    own_b = own_weight.astype(jnp.bfloat16).astype(jnp.float32)
    summed = summed + own_b[:, :, None] * own_key[:, None, :latent_width].astype(jnp.float32)
    return (summed / total[:, :, None]).astype(jnp.bfloat16)


def per_device(
    kv_pages,
    page_dest,
    page_req,
    page_fill,
    queries,
    new_latent,
    moe_in,
    route_ids,
    route_w,
    w_gate,
    w_up,
    w_down,
):
    n_grp = lax.axis_size("grp")
    target = lax.axis_index("grp")
    column = lax.axis_index("ep")
    pages_dev = kv_pages.shape[0]
    page = kv_pages.shape[1]
    width = kv_pages.shape[2]
    cap = max(2, (pages_dev + n_grp - 1) // n_grp)
    dest = page_dest[0, :, 0].reshape(n_grp, pages_dev)
    ranks = page_ranks(dest, n_grp)
    my_dest = lax.dynamic_index_in_dim(dest, target, 0, False)
    my_rank = lax.dynamic_index_in_dim(ranks, target, 0, False)
    groups = jnp.arange(n_grp, dtype=jnp.int32)
    slots = jnp.arange(cap, dtype=jnp.int32)
    outward = (my_dest[None, None, :] == groups[:, None, None]) & (
        my_rank[None, None, :] == slots[None, :, None]
    )
    outward = outward.astype(jnp.int32)
    pick = jnp.sum(outward * jnp.arange(pages_dev, dtype=jnp.int32)[None, None, :], axis=2)
    used = jnp.sum(outward, axis=2)
    outgoing = jnp.take(kv_pages, pick.reshape(-1), axis=0).reshape(n_grp, cap, page, width)
    outgoing = outgoing * used[:, :, None, None].astype(jnp.bfloat16)
    arrived = lax.all_to_all(outgoing, "grp", split_axis=0, concat_axis=0, tiled=True)
    inward = ((dest == target)[:, :, None] & (ranks[:, :, None] == slots[None, None, :])).astype(
        jnp.int32
    )
    req_tab = page_req[0].reshape(n_grp, pages_dev)
    fill_tab = page_fill[0].reshape(n_grp, pages_dev)
    slot_req = jnp.sum(inward * req_tab[:, :, None], axis=1).reshape(-1)
    slot_fill = jnp.sum(inward * fill_tab[:, :, None], axis=1).reshape(-1)
    attn_latent = attend(
        queries, new_latent, arrived.reshape(-1, page, width), slot_req, slot_fill, KV_L
    )
    moe_out = moe_call(moe_in, route_ids, route_w, w_gate, w_up, w_down)
    return (attn_latent, moe_out)


def solution(mesh):
    return jax.shard_map(
        per_device,
        mesh=mesh,
        in_specs=(
            P(("grp", "ep"), None, None),
            P("ep", None, None),
            P("ep", None),
            P("ep", None),
            P(("grp", "ep"), None, None),
            P(("grp", "ep"), None),
            P(("grp", "ep"), None),
            P(("grp", "ep"), None),
            P(("grp", "ep"), None),
            P("ep", "grp", None),
            P("ep", "grp", None),
            P("ep", "grp", None),
        ),
        out_specs=(P(("grp", "ep"), None, None), P(("grp", "ep"), None)),
        check_vma=False,
    )
```

```python
import functools

import jax
import jax.numpy as jnp
from jax import lax
from jax.experimental import pallas as pl
from jax.experimental.pallas import tpu as pltpu
from jax.sharding import PartitionSpec as P

MESH = pl.DeviceIdType.MESH
EXPERTS = 16
HALF = 3584
QUART = 1792
SPLIT = ((0, 2688), (2688, 896))
PLACE = (0, 2, 3, 1)
GW = HALF + 128
BF = jnp.bfloat16
F32 = jnp.float32


def coords():
    g = lax.axis_index("grp")
    e = lax.axis_index("ep")
    return (g // 16) * 2 + e % 2, e // 2, (g // 2) % 8, g % 2


def device(x, y, z, c):
    x, y, z, c = (x + 4) % 4, (y + 4) % 4, (z + 8) % 8, (c + 2) % 2
    return ((x // 2) * 16 + z * 2 + c, y * 2 + x % 2)


def ring_member(x, y, m):
    m = (m + 16) % 16
    return device(x, y, m // 2, m % 2)


def greet(partners):
    sem = pltpu.get_barrier_semaphore()
    for p in partners:
        pl.semaphore_signal(sem, 1, device_id=p, device_id_type=MESH)


def dot_t(a, b):
    return lax.dot_general(a, b, (((1,), (1,)), ((), ())), preferred_element_type=F32)


def moe_steps(r):
    x, y, z, c = coords()
    m = z * 2 + c
    mate = device(x, y, z, 1 - c)

    def push(src, dst, ss, rs, dev):
        cp = pltpu.make_async_remote_copy(src, dst, ss, rs, device_id=dev, device_id_type=MESH)
        cp.start()
        return cp

    loads = [
        pltpu.make_async_copy(r["wg"], r["w1"].at[pl.ds(0, 128)], r["lsem"].at[0]),
        pltpu.make_async_copy(r["wu"], r["w1"].at[pl.ds(128, 128)], r["lsem"].at[1]),
        pltpu.make_async_copy(r["wd"], r["w2"], r["lsem"].at[2]),
    ]
    tok, ra = r["tok"], r["ra"]
    cps = []
    for k in range(1, 16):
        mm = (m + k) % 16
        cps.append(push(tok.at[mm % 2], ra.at[m], r["sa"].at[0, k], r["sa"].at[1, k], ring_member(x, y, mm)))
    for cp in loads:
        cp.start()
    ra[m] = tok[c]
    yield
    for cp in cps:
        cp.wait()
    rows = lax.broadcasted_iota(jnp.int32, (464, 512), 0)
    cols = lax.broadcasted_iota(jnp.int32, (464, 512), 1)
    pick = jnp.where(cols == (rows % 16) * 32 + rows // 16, 1.0, 0.0).astype(BF)
    got = jnp.dot(pick, ra[...].reshape(512, 128), preferred_element_type=F32).astype(BF)
    xb = r["xb"]
    mine = y * 4 + x
    for j in range(29):
        xb[c, mine, :, j * 128 : (j + 1) * 128] = got[j * 16 : (j + 1) * 16]
    up, down = device(x, y + 1, z, c), device(x, y - 1, z, c)

    def block(ky, kx):
        return ((y - ky + 4) % 4) * 4 + (x - kx + 4) % 4

    bcp, ccp, dcp = {}, {}, {}

    def to_mate(ky):
        blk = xb.at[c, pl.ds(((y - ky + 4) % 4) * 4, 4)]
        dcp[ky] = push(blk, blk, r["sd"].at[0, ky], r["sd"].at[1, ky], mate)

    def along_y(kx):
        blk = xb.at[c, block(0, kx)]
        ccp[1, kx] = push(blk, blk, r["sc"].at[0, 1, kx], r["sc"].at[1, 1, kx], up)
        ccp[3, kx] = push(blk, blk, r["sc"].at[0, 3, kx], r["sc"].at[1, 3, kx], down)

    blk = xb.at[c, mine]
    for k in (1, 3, 2):
        bcp[k] = push(blk, blk, r["sb"].at[0, k], r["sb"].at[1, k], device(x + k, y, z, c))
    along_y(0)
    yield
    for k in (1, 3):
        bcp[k].wait()
        along_y(k)
    yield
    bcp[2].wait()
    along_y(2)
    to_mate(0)
    yield
    for kx in (0, 1, 3, 2):
        for ky in (1, 3):
            ccp[ky, kx].wait()
            if (ky == 1) == (kx in (0, 2)):
                blk = xb.at[c, block(ky, kx)]
                ccp[2, kx] = push(blk, blk, r["sc"].at[0, 2, kx], r["sc"].at[1, 2, kx], up if ky == 1 else down)
        if kx in (1, 3):
            yield
    to_mate(1)
    to_mate(3)
    yield
    w1, w2, acc = r["w1"], r["w2"], r["acc"]

    def first_products(kys, row):
        n = 64 * len(kys)
        for h in range(2):
            for q in range(2):
                at = q * QUART
                a = jnp.concatenate(
                    [xb[h, pl.ds(((y - ky + 4) % 4) * 4, 4), :, at : at + QUART].reshape(64, QUART) for ky in kys], axis=0
                )
                p = dot_t(a, w1[:, h * HALF + at : h * HALF + at + QUART])
                if h + q == 0:
                    acc[row : row + n] = p
                else:
                    acc[row : row + n] += p

    for ky in (0, 1, 3):
        dcp[ky].wait()
    for cp in loads:
        cp.wait()
    first_products((0, 1, 3), 0)
    yield
    for kx in (0, 1, 3, 2):
        ccp[2, kx].wait()
    to_mate(2)
    yield
    dcp[2].wait()
    first_products((2,), 192)
    first, second = acc[:, :128], acc[:, 128:]
    hidden = ((first / (1.0 + jnp.exp(-first))) * second).astype(BF).astype(F32)
    gates = jnp.concatenate(
        [xb[0, pl.ds(((y - ky + 4) % 4) * 4, 4), :, HALF:].reshape(64, 128) for ky in (0, 1, 3, 2)], axis=0
    ).astype(F32)
    col = lax.axis_index("ep")
    lane = lax.broadcasted_iota(jnp.int32, (256, 128), 1)
    g0 = jnp.sum(jnp.where(lane == col * 2, gates, 0.0), axis=1, keepdims=True)
    g1 = jnp.sum(jnp.where(lane == col * 2 + 1, gates, 0.0), axis=1, keepdims=True)
    scaled = hidden * jnp.where(lane < 64, g0, g1)
    hi = scaled.astype(BF)
    lo = (scaled - hi.astype(F32)).astype(BF)
    ybf, yown, rc = r["ybf"], r["yown"], r["rc"]
    hl = jnp.concatenate([hi, lo], axis=1)

    def second_product(h, store):
        def step(k, carry):
            at = pl.multiple_of(k * 512, 512)
            w = w2[:, pl.ds(pl.multiple_of(h * HALF + at, 128), 512)]
            out = jnp.dot(hl, jnp.concatenate([w, w], axis=0), preferred_element_type=F32)
            store(at, out.reshape(4, 4, 16, 512))
            return carry

        lax.fori_loop(0, 7, step, 0)

    def keep_bf(at, v):
        ybf[:, :, :, pl.ds(at, 512)] = v.astype(BF)

    def to_own(at, v):
        yown[:, :, :, pl.ds(at, 512)] = v

    second_product(1 - c, keep_bf)
    cps = {i: push(ybf.at[i], rc.at[i], r["se"].at[0, i], r["se"].at[1, i], mate) for i in (3, 2, 1, 0)}
    second_product(c, to_own)
    yield
    s2, r2, yacc = [r["s2a"], r["s2b"]], [r["r2a"], r["r2b"]], [r["yacca"], r["yaccb"]]

    def share(p, k, blk):
        def step(q, carry):
            at = pl.multiple_of(q * 896, 128)
            cols = pl.ds(pl.multiple_of(SPLIT[p][0] + at, 128), 896)
            if p == 0:
                v = yown[blk, :, :, cols] + rc[blk, :, :, cols].astype(F32)
            else:
                v = yown[:, blk, :, cols] + rc[:, blk, :, cols].astype(F32)
            if k == 0:
                yacc[p][:, :, pl.ds(at, 896)] = v
            else:
                s2[p][k - 1, :, :, pl.ds(at, 896)] = v.astype(BF)
            return carry

        lax.fori_loop(0, SPLIT[p][1] // 896, step, 0)

    def far_side(p, k):
        return device(x, y + k, z, c) if p == 0 else device(x + k, y, z, c)

    fcps = {}
    for k in (2, 1, 3):
        cps[PLACE[k]].wait()
        share(0, k, PLACE[k])
        fcps[0, k] = push(s2[0].at[k - 1], r2[0].at[k - 1], r["sf"].at[0, 0, k], r["sf"].at[1, 0, k], far_side(0, k))
    cps[0].wait()
    for k in (2, 1, 3):
        share(1, k, (x + k) % 4)
        fcps[1, k] = push(s2[1].at[k - 1], r2[1].at[k - 1], r["sf"].at[0, 1, k], r["sf"].at[1, 1, k], far_side(1, k))
    share(0, 0, 0)
    share(1, 0, x)
    yield
    s3, r3, zacc = [r["s3a"], r["s3b"]], [r["r3a"], r["r3b"]], [r["zacca"], r["zaccb"]]
    gcps = {}
    for p in range(2):
        for k in (1, 3, 2):
            fcps[p, k].wait()
        for k in (2, 1, 3, 0):
            b = PLACE[k] if p else (x + k) % 4
            v = yacc[p][b]
            for i in range(3):
                v = v + r2[p][i, b].astype(F32)
            if k == 0:
                zacc[p][...] = v
            else:
                s3[p][k - 1] = v.astype(BF)
                gcps[p, k] = push(s3[p].at[k - 1], r3[p].at[k - 1], r["sg"].at[0, p, k], r["sg"].at[1, p, k], far_side(1 - p, k))
    yield
    for cp in gcps.values():
        cp.wait()
    parts = []
    for p in range(2):
        v = zacc[p][...]
        for i in range(3):
            v = v + r3[p][i].astype(F32)
        parts.append(v)
    v = jnp.concatenate(parts, axis=1)
    vb = v.astype(BF)
    stack = jnp.concatenate([vb[:, j * 128 : (j + 1) * 128] for j in range(28)], axis=0)
    rows = lax.broadcasted_iota(jnp.int32, (512, 448), 0)
    cols = lax.broadcasted_iota(jnp.int32, (512, 448), 1)
    pick = jnp.where(cols == (rows % 32) * 16 + rows // 32, 1.0, 0.0).astype(BF)
    t4, r4 = r["t4"], r["r4"]
    t4[...] = jnp.dot(pick, stack, preferred_element_type=F32).astype(BF).reshape(16, 32, 128)
    cps = []
    for k in range(1, 16):
        mm = (m + k) % 16
        cps.append(push(t4.at[mm], r4.at[m], r["sh"].at[0, k], r["sh"].at[1, k], ring_member(x, y, mm)))
    r4[m] = t4[m]
    yield
    for cp in cps:
        cp.wait()
    row = []
    for h in range(2):
        tot = r4[h].astype(F32)
        for i in range(1, 8):
            tot = tot + r4[2 * i + h].astype(F32)
        row += [tot[j : j + 1] for j in range(28)]
    r["mo"][...] = jnp.concatenate(row, axis=1).astype(BF)


MOE_SCRATCH = dict(
    w1=pltpu.VMEM((256, 2 * HALF), BF),
    w2=pltpu.VMEM((128, 2 * HALF), BF),
    ra=pltpu.VMEM((16, 32, 128), BF),
    xb=pltpu.VMEM((2, 16, 16, GW), BF),
    acc=pltpu.VMEM((256, 256), F32),
    ybf=pltpu.VMEM((4, 4, 16, HALF), BF),
    yown=pltpu.VMEM((4, 4, 16, HALF), F32),
    rc=pltpu.VMEM((4, 4, 16, HALF), BF),
    s2a=pltpu.VMEM((3, 4, 16, 2688), BF),
    s2b=pltpu.VMEM((3, 4, 16, 896), BF),
    r2a=pltpu.VMEM((3, 4, 16, 2688), BF),
    r2b=pltpu.VMEM((3, 4, 16, 896), BF),
    yacca=pltpu.VMEM((4, 16, 2688), F32),
    yaccb=pltpu.VMEM((4, 16, 896), F32),
    s3a=pltpu.VMEM((3, 16, 2688), BF),
    s3b=pltpu.VMEM((3, 16, 896), BF),
    r3a=pltpu.VMEM((3, 16, 2688), BF),
    r3b=pltpu.VMEM((3, 16, 896), BF),
    zacca=pltpu.VMEM((16, 2688), F32),
    zaccb=pltpu.VMEM((16, 896), F32),
    t4=pltpu.VMEM((16, 32, 128), BF),
    r4=pltpu.VMEM((16, 32, 128), BF),
    lsem=pltpu.SemaphoreType.DMA((3,)),
    sa=pltpu.SemaphoreType.DMA((2, 16)),
    sb=pltpu.SemaphoreType.DMA((2, 4)),
    sc=pltpu.SemaphoreType.DMA((2, 4, 4)),
    sd=pltpu.SemaphoreType.DMA((2, 4)),
    se=pltpu.SemaphoreType.DMA((2, 4)),
    sf=pltpu.SemaphoreType.DMA((2, 2, 4)),
    sg=pltpu.SemaphoreType.DMA((2, 2, 4)),
    sh=pltpu.SemaphoreType.DMA((2, 16)),
)


def moe_partners():
    x, y, z, c = coords()
    m = z * 2 + c
    out = [ring_member(x, y, m + k) for k in range(1, 16)]
    out += [device(x + k, y, z, c) for k in (1, 2, 3)]
    out += [device(x, y + k, z, c) for k in (1, 2, 3)]
    return out


SCALE = 192.0 ** (-0.5)
NEG = -1e30
KV_L = 512
ORDER = (4, 3, -3, 2, -2, 1, -1, 0)


def lane_of(s):
    return s // 2, s % 2


def attn_steps(r):
    x, y, z, c = coords()
    xh, xl = x // 2, x % 2
    own = xh * 2 + c
    right, left = device(x, y, z + 1, c), device(x, y, z - 1, c)
    ahead = (right, left)

    def push(src, dst, sems, at, dev):
        cp = pltpu.make_async_remote_copy(src, dst, sems.at[(0, *at)], sems.at[(1, *at)], device_id=dev, device_id_type=MESH)
        cp.start()
        return cp

    qin, kvv, pick, mask, nl = r["q"], r["kvv"], r["pick"], r["mask"], r["nl"]
    ql, kl, ol = r["ql"], r["kl"], r["ol"]
    r["qcp"].wait()
    for i in range(2):
        ql[0, i * 160 : i * 160 + 128] = qin[i, :KV_L].astype(F32).T.astype(BF)
    rope = jnp.concatenate([qin[0, KV_L:].astype(F32), qin[1, KV_L:].astype(F32)], axis=0).T.astype(BF)
    for i in range(4):
        ql[0, 128:160, i * 128 : (i + 1) * 128] = rope[i * 32 : (i + 1) * 32]
    qcp = {}

    def send_q(d, hop):
        at = 0 if hop == 0 else 1 + d * 3 + hop - 1
        to = 1 + d * 3 + hop
        qcp[d, hop + 1] = push(ql.at[at], ql.at[to], r["sq"], (d, hop), ahead[d])

    def send_q4(d):
        at = 1 + d * 3 + 2
        rows = pl.ds(160, 128) if d else pl.ds(0, 160)
        qcp[d, 4] = push(ql.at[at, rows], ql.at[7, rows], r["sq"], (d, 3), ahead[d])

    xcp, lcp = r["xcp"], r["lcp"]

    def gather(i):
        zt = (z + ORDER[i] + 8) % 8

        def copy_page(n, carry):
            k, t = n // 2, n % 2
            to = ((xh + k // 2) % 2) * 16 + zt * 2 + (c + k) % 2
            page = kvv[pick[t, to]]
            at = pl.multiple_of(t * 32, 32)
            ol[i, k, pl.ds(at, 32)] = page[:32, :KV_L]
            ol[i, k, pl.ds(at + 64, 32)] = page[32:, :KV_L]
            rope = jnp.concatenate([page[:32, KV_L:], page[32:, KV_L:]], axis=1)
            for j in range(2):
                ol[i, k, 128:144, pl.ds(pl.multiple_of((t * 2 + j) * 128, 128), 128)] = rope[j * 16 : (j + 1) * 16]
            return carry

        lax.fori_loop(0, 8, copy_page, 0)

    r["kvcp"].wait()
    for i in range(8):
        gather(i)
    yield
    send_q(0, 0)
    send_q(1, 0)
    yield
    for hop in (1, 2, 3):
        for d in (0, 1):
            qcp[d, hop].wait()
            if hop < 3:
                send_q(d, hop)
            else:
                send_q4(d)
        yield
    lane = lax.broadcasted_iota(jnp.int32, (128, 128), 1)
    pacc, pm, ps = r["pacc"], r["pm"], r["ps"]
    ca, cs, sa, ss = r["ca"], r["cs"], r["cout"], r["csout"]

    def rope_of(at):
        return jnp.concatenate([ql[at, 128:160, j * 128 : (j + 1) * 128] for j in range(4)], axis=0)

    def partial(i, at):
        q = jnp.concatenate([ql[at, :128], ql[at, 160:]], axis=0)
        a = rope_of(at).astype(F32)
        b = pltpu.roll(a, 64, 1)
        lo = jnp.concatenate([jnp.where(lane < 64, a, 0.0), jnp.where(lane < 64, b, 0.0)], axis=0).astype(BF)
        hi = jnp.concatenate([jnp.where(lane >= 64, b, 0.0), jnp.where(lane >= 64, a, 0.0)], axis=0).astype(BF)
        kv = jnp.concatenate(
            [kl[i, n, 128:144, j * 128 : (j + 1) * 128] for n in range(4) for j in range(4)], axis=0
        )
        near, far = kl[i, :, :64].reshape(256, KV_L), kl[i, :, 64:128].reshape(256, KV_L)
        s = jnp.concatenate(
            [
                dot_t(q, near) + dot_t(lo, kv),
                dot_t(q, far) + dot_t(hi, kv),
            ],
            axis=1,
        ) * SCALE
        live = jnp.concatenate(
            [jnp.broadcast_to(mask[h, i : i + 1], (128, 512)) for h in range(2)], axis=0
        ) > 0.5
        peak = jnp.max(jnp.where(live, s, NEG), axis=1, keepdims=True)
        w = jnp.where(live, jnp.exp(s - peak), 0.0)
        pm[...] = jnp.broadcast_to(peak, (256, 128))
        ps[...] = jnp.broadcast_to(jnp.sum(w, axis=1, keepdims=True), (256, 128))
        wb = w.astype(BF)
        pacc[...] = jnp.dot(wb[:, :256], near, preferred_element_type=F32) + jnp.dot(
            wb[:, 256:], far, preferred_element_type=F32
        )

    def mine(i):
        rows = pl.ds(i * 128, 128)
        return pm[rows, 0:1], ps[rows, 0:1], pacc[rows]

    def merge(a, b):
        peak = jnp.maximum(a[0], b[0])
        u, v = jnp.exp(a[0] - peak), jnp.exp(b[0] - peak)
        return peak, a[1] * u + b[1] * v, a[2] * u + b[2] * v

    ccp = {}

    def send_part(d, dist, i, part):
        at = (d * 4 + dist - 1) * 2 + i
        sa[at] = part[2].astype(BF)
        ss[at] = jnp.where(lane == 0, part[0], part[1]).T[:8]
        ccp[d, dist, i] = [
            push(sa.at[at], ca.at[at], r["sch"], (0, at), ahead[d]),
            push(ss.at[at], cs.at[at], r["sch"], (1, at), ahead[d]),
        ]

    def came(d, dist, i):
        for cp in ccp[d, dist, i]:
            cp.wait()
        at = (d * 4 + dist - 1) * 2 + i
        st = jnp.concatenate([cs[at]] * 16, axis=0).T
        return st[:, 0:1], st[:, 1:2], ca[at].astype(F32)

    for i, dz in enumerate(ORDER):
        r["ready"](i)
        for k in (2, 3, 1):
            xcp[i, k].wait_recv()
        lcp[i].wait()
        if dz == 4:
            for d in (0, 1):
                qcp[d, 4].wait()
            partial(i, 7)
            for d in (0, 1):
                send_part(d, 4, d, mine(d))
            yield
            continue
        if dz:
            d = 0 if dz > 0 else 1
            at = 1 + (1 - d) * 3 + abs(dz) - 1
            partial(i, at)
            yield
            for part in (d, 1 - d):
                v = mine(part)
                if abs(dz) < 3 or part == d:
                    v = merge(came(d, abs(dz) + 1, part), v)
                send_part(d, abs(dz), part, v)
            yield
            continue
        partial(i, 0)
        own_rope = jnp.concatenate([nl[0:1, KV_L:], nl[1:2, KV_L:]], axis=1).astype(F32)
        for part in range(2):
            key = nl[part : part + 1].astype(F32)
            qv = ql[0, part * 160 : part * 160 + 128].astype(F32)
            rope = jnp.where(lane // 64 == part, rope_of(0).astype(F32) * own_rope, 0.0)
            score = (jnp.sum(qv * key[:, :KV_L], axis=1, keepdims=True) + jnp.sum(rope, axis=1, keepdims=True)) * SCALE
            m0, s0, a0 = mine(part)
            peak = jnp.maximum(m0, score)
            u, w = jnp.exp(m0 - peak), jnp.exp(score - peak)
            rows = pl.ds(part * 128, 128)
            pacc[rows] = a0 * u + w.astype(BF).astype(F32) * key[:, :KV_L]
            ps[rows] = jnp.broadcast_to(s0 * u + w, (128, 128))
            pm[rows] = jnp.broadcast_to(peak, (128, 128))
        yield
        for part in range(2):
            v = mine(part)
            v = merge(v, came(0, 1, part))
            v = merge(v, came(1, 1, part))
            r["ao"][part] = (v[2] / v[1]).astype(BF)


def page_steps(r):
    x, y, z, c = coords()
    own = (x // 2) * 2 + c
    ol, kl, xcp, lcp = r["ol"], r["kl"], r["xcp"], r["lcp"]

    def push(src, dst, at, dev):
        cp = pltpu.make_async_remote_copy(src, dst, r["sx"].at[(0, *at)], r["sx"].at[(1, *at)], device_id=dev, device_id_type=MESH)
        cp.start()
        return cp

    for i in range(8):
        for k in (2, 3, 1):
            to = device(x + 2 * (k // 2), y, z, c + k % 2)
            xcp[i, k] = push(ol.at[i, k], kl.at[i, own], (i, k), to)
        lcp[i] = pltpu.make_async_copy(ol.at[i, 0], kl.at[i, own], r["sl"].at[i])
        lcp[i].start()
        yield
    for cp in xcp.values():
        cp.wait_send()


ATTN_SCRATCH = dict(
    q=pltpu.VMEM((2, 576, 128), BF),
    kvv=pltpu.VMEM((32, 64, 576), BF),
    ql=pltpu.VMEM((8, 288, 512), BF),
    kl=pltpu.VMEM((8, 4, 144, 512), BF),
    ol=pltpu.VMEM((8, 4, 144, 512), BF),
    pacc=pltpu.VMEM((256, 512), F32),
    pm=pltpu.VMEM((256, 128), F32),
    ps=pltpu.VMEM((256, 128), F32),
    ca=pltpu.VMEM((16, 128, 512), BF),
    cs=pltpu.VMEM((16, 8, 128), F32),
    cout=pltpu.VMEM((16, 128, 512), BF),
    csout=pltpu.VMEM((16, 8, 128), F32),
    skv=pltpu.SemaphoreType.DMA,
    sqin=pltpu.SemaphoreType.DMA,
    sq=pltpu.SemaphoreType.DMA((2, 2, 4)),
    sx=pltpu.SemaphoreType.DMA((2, 8, 4)),
    sl=pltpu.SemaphoreType.DMA((8,)),
    sch=pltpu.SemaphoreType.DMA((2, 2, 16)),
)


def attn_partners():
    x, y, z, c = coords()
    return [
        device(x, y, z + 1, c),
        device(x, y, z - 1, c),
        device(x, y, z, 1 - c),
        device(x + 2, y, z, c),
        device(x + 2, y, z, 1 - c),
    ]


def tables_kernel(dest, req, fill, mi, ids, rw, pick, mask, tok, tf):
    g = lax.axis_index("grp")
    xh, z, c = g // 16, (g // 2) % 8, g % 2
    x = mi[...].astype(F32)
    lane = lax.broadcasted_iota(jnp.int32, (1, 128), 1)
    gates = jnp.zeros((1, 128), F32)
    for k in range(8):
        gates = gates + jnp.where(lane == ids[:, k : k + 1], rw[:, k : k + 1], 0.0)
    for h in range(2):
        for j in range(28):
            tf[h, j : j + 1] = x[:, (h * 28 + j) * 128 : (h * 28 + j + 1) * 128]
        tf[h, 28:29] = gates
        tf[h, 29:32] = jnp.zeros((3, 128), F32)
    tok[...] = tf[...].astype(BF)
    rows = lax.broadcasted_iota(jnp.int32, (128, 128), 0)
    cols = lax.broadcasted_iota(jnp.int32, (128, 128), 1)
    earlier = jnp.where((rows // 32 == cols // 32) & (cols < rows), 1.0, 0.0).astype(BF)
    code, found = [], []
    for xs in range(2):
        at = pl.multiple_of((xs * 4 + z // 2) * 128, 128)
        value = (fill[:, pl.ds(at, 128)] + 128 * req[:, pl.ds(at, 128)]).astype(F32)
        quarter = lane // 32 - (z % 2) * 2
        left = jnp.concatenate(
            [
                jnp.where(quarter == 0, value, 0.0),
                jnp.where(quarter == 1, value, 0.0),
                jnp.where(quarter == c, (lane % 32).astype(F32), 0.0),
                jnp.zeros((13, 128), F32),
            ],
            axis=0,
        ).astype(BF)
        goes = jnp.broadcast_to(dest[:, pl.ds(at, 128)].astype(F32), (128, 128)).T == cols.astype(F32)
        onehot = jnp.where(goes, 1.0, 0.0).astype(BF)
        before = jnp.dot(earlier, onehot, preferred_element_type=F32)
        at_rank = [
            jnp.dot(left, jnp.where(goes & (before == t), 1.0, 0.0).astype(BF), preferred_element_type=F32)
            for t in range(2)
        ]
        for cc in range(2):
            for t in range(2):
                code.append(at_rank[t][cc : cc + 1])
        found.append([v[2:3] for v in at_rank])
    pick[...] = jnp.concatenate(
        [jnp.where(xh == 0, found[0][t], found[1][t]).astype(jnp.int32) for t in range(2)], axis=0
    )
    codes = jnp.concatenate(code + [jnp.zeros((120, 128), F32)], axis=0).astype(BF)
    plane = lax.broadcasted_iota(jnp.int32, (16, 128), 0)
    away = jnp.zeros((16, 128), jnp.int32)
    for i, dz in enumerate(ORDER):
        away = jnp.where(plane == i, dz, away)
    target = xh * 16 + ((z + away + 8) % 8) * 2 + c
    goal = jnp.where(lax.broadcasted_iota(jnp.int32, (16, 128), 1) == target, 1.0, 0.0).astype(BF)
    slot = dot_t(goal, codes).astype(BF)
    key = lax.broadcasted_iota(jnp.int32, (128, 512), 1)
    spread = jnp.where((key // 32) % 8 == lax.broadcasted_iota(jnp.int32, (128, 512), 0), 1.0, 0.0).astype(BF)
    full = jnp.dot(slot, spread, preferred_element_type=F32)[:8]
    key = lax.broadcasted_iota(jnp.int32, (8, 512), 1)
    pos = ((key // 256) * 32 + key % 32).astype(F32)
    second = full >= 128.0
    mask[0] = jnp.where((pos < full) & ~second, 1.0, 0.0)
    mask[1] = jnp.where((pos < full - 128.0) & second, 1.0, 0.0)


SCHEDULE = "mskmkkksmmskkkkmsmmmsmsmsssssmssssmssmmss"


def merged_kernel(schedule, pick, kv, q, mask, nl, tok, wg, wu, wd, ao, mo, *scratch):
    n = len(ATTN_SCRATCH)
    ra = dict(zip(ATTN_SCRATCH, scratch[:n]), pick=pick, mask=mask, nl=nl, ao=ao)
    rm = dict(zip(MOE_SCRATCH, scratch[n:]), tok=tok, wg=wg, wu=wu, wd=wd, mo=mo)
    ra["kvcp"] = pltpu.make_async_copy(kv, ra["kvv"], ra["skv"])
    qcp = pltpu.make_async_copy(q, ra["q"], ra["sqin"])
    ra["qcp"] = qcp
    ra["kvcp"].start()
    qcp.start()
    ra["xcp"], ra["lcp"] = {}, {}
    steps = {"s": attn_steps(ra), "m": moe_steps(rm), "k": page_steps(ra)}

    def ready(i):
        while i not in ra["lcp"]:
            next(steps["k"])

    ra["ready"] = ready
    partners = moe_partners() + attn_partners()[-1:]
    greet(partners)
    next(steps["s"])
    pl.semaphore_wait(pltpu.get_barrier_semaphore(), len(partners))
    for s in schedule:
        next(steps[s], None)
    for s in "smk":
        for _ in steps[s]:
            pass


def merged_call(kv_pages, page_dest, page_req, page_fill, queries, new_latent, moe_in, route_ids, route_w, w_gate, w_up, w_down):
    vm = pl.BlockSpec(memory_space=pltpu.VMEM)
    hb = pl.BlockSpec(memory_space=pl.ANY)
    pick, mask, tok = pl.pallas_call(
        tables_kernel,
        name="tables",
        out_shape=(
            jax.ShapeDtypeStruct((2, 128), jnp.int32),
            jax.ShapeDtypeStruct((2, 8, 512), F32),
            jax.ShapeDtypeStruct((2, 32, 128), BF),
        ),
        in_specs=[vm] * 6,
        out_specs=(vm, vm, vm),
        scratch_shapes=[
            pltpu.VMEM((2, 32, 128), F32),
        ],
    )(jnp.swapaxes(page_dest, 1, 2).reshape(1, -1), page_req, page_fill, moe_in, route_ids, route_w)
    return pl.pallas_call(
        functools.partial(merged_kernel, SCHEDULE),
        name="decode",
        out_shape=(jax.ShapeDtypeStruct((2, 128, KV_L), BF), jax.ShapeDtypeStruct((1, 2 * HALF), BF)),
        in_specs=[pl.BlockSpec(memory_space=pltpu.SMEM), hb, hb, vm, vm, vm, hb, hb, hb],
        out_specs=(vm, vm),
        scratch_shapes=list(ATTN_SCRATCH.values()) + list(MOE_SCRATCH.values()),
        compiler_params=pltpu.CompilerParams(collective_id=0, has_side_effects=True, vmem_limit_bytes=60 * 2**20),
    )(pick, kv_pages, jnp.swapaxes(queries, 1, 2), mask, new_latent, tok, w_gate.reshape(128, -1), w_up.reshape(128, -1), w_down.reshape(128, -1))


def solution(mesh):
    return jax.shard_map(
        merged_call,
        mesh=mesh,
        in_specs=(
            P(("grp", "ep"), None, None),
            P("ep", None, None),
            P("ep", None),
            P("ep", None),
            P(("grp", "ep"), None, None),
            P(("grp", "ep"), None),
            P(("grp", "ep"), None),
            P(("grp", "ep"), None),
            P(("grp", "ep"), None),
            P("ep", "grp", None),
            P("ep", "grp", None),
            P("ep", "grp", None),
        ),
        out_specs=(P(("grp", "ep"), None, None), P(("grp", "ep"), None)),
        check_vma=False,
    )
```

```python
import functools

import jax
import jax.numpy as jnp
from jax import lax
from jax.experimental import pallas as pl
from jax.experimental.pallas import tpu as pltpu
from jax.sharding import PartitionSpec as P

MESH = pl.DeviceIdType.MESH
EXPERTS = 16
HALF = 3584
QUART = 1792
SPLIT = ((0, 3072), (3072, 512))
PLACE = (0, 2, 3, 1)
GW = HALF + 128
BF = jnp.bfloat16
F32 = jnp.float32


def coords():
    g = lax.axis_index("grp")
    e = lax.axis_index("ep")
    return (g // 16) * 2 + e % 2, e // 2, (g // 2) % 8, g % 2


def device(x, y, z, c):
    x, y, z, c = (x + 4) % 4, (y + 4) % 4, (z + 8) % 8, (c + 2) % 2
    return ((x // 2) * 16 + z * 2 + c, y * 2 + x % 2)


def ring_member(x, y, m):
    m = (m + 16) % 16
    return device(x, y, m // 2, m % 2)


def greet(partners):
    sem = pltpu.get_barrier_semaphore()
    for p in partners:
        pl.semaphore_signal(sem, 1, device_id=p, device_id_type=MESH)


def dot_t(a, b):
    return lax.dot_general(a, b, (((1,), (1,)), ((), ())), preferred_element_type=F32)


def moe_steps(r):
    x, y, z, c = coords()
    m = z * 2 + c
    mate = device(x, y, z, 1 - c)

    def push(src, dst, ss, rs, dev):
        cp = pltpu.make_async_remote_copy(src, dst, ss, rs, device_id=dev, device_id_type=MESH)
        cp.start()
        return cp

    loads = [
        pltpu.make_async_copy(r["wg"], r["w1"].at[pl.ds(0, 128)], r["lsem"].at[0]),
        pltpu.make_async_copy(r["wu"], r["w1"].at[pl.ds(128, 128)], r["lsem"].at[1]),
        pltpu.make_async_copy(r["wd"], r["w2"], r["lsem"].at[2]),
    ]
    tok, ra = r["tok"], r["ra"]
    cps = []
    for k in range(1, 16):
        mm = (m + k) % 16
        cps.append(push(tok.at[mm % 2], ra.at[m], r["sa"].at[0, k], r["sa"].at[1, k], ring_member(x, y, mm)))
    for cp in loads:
        cp.start()
    ra[m] = tok[c]
    yield
    for cp in cps:
        cp.wait()
    rows = lax.broadcasted_iota(jnp.int32, (464, 512), 0)
    cols = lax.broadcasted_iota(jnp.int32, (464, 512), 1)
    pick = jnp.where(cols == (rows % 16) * 32 + rows // 16, 1.0, 0.0).astype(BF)
    got = jnp.dot(pick, ra[...].reshape(512, 128), preferred_element_type=F32).astype(BF)
    xb = r["xb"]
    mine = y * 4 + x
    for j in range(29):
        xb[c, mine, :, j * 128 : (j + 1) * 128] = got[j * 16 : (j + 1) * 16]
    up, down = device(x, y + 1, z, c), device(x, y - 1, z, c)

    def block(ky, kx):
        return ((y - ky + 4) % 4) * 4 + (x - kx + 4) % 4

    bcp, ccp, dcp = {}, {}, {}

    def to_mate(ky):
        blk = xb.at[c, pl.ds(((y - ky + 4) % 4) * 4, 4)]
        dcp[ky] = push(blk, blk, r["sd"].at[0, ky], r["sd"].at[1, ky], mate)

    def along_y(kx):
        blk = xb.at[c, block(0, kx)]
        ccp[1, kx] = push(blk, blk, r["sc"].at[0, 1, kx], r["sc"].at[1, 1, kx], up)
        ccp[3, kx] = push(blk, blk, r["sc"].at[0, 3, kx], r["sc"].at[1, 3, kx], down)

    blk = xb.at[c, mine]
    for k in (1, 3, 2):
        bcp[k] = push(blk, blk, r["sb"].at[0, k], r["sb"].at[1, k], device(x + k, y, z, c))
    along_y(0)
    yield
    for k in (1, 3):
        bcp[k].wait()
        along_y(k)
    yield
    bcp[2].wait()
    along_y(2)
    to_mate(0)
    yield
    for kx in (0, 1, 3, 2):
        for ky in (1, 3):
            ccp[ky, kx].wait()
            if (ky == 1) == (kx in (0, 2)):
                blk = xb.at[c, block(ky, kx)]
                ccp[2, kx] = push(blk, blk, r["sc"].at[0, 2, kx], r["sc"].at[1, 2, kx], up if ky == 1 else down)
        if kx in (1, 3):
            yield
    to_mate(1)
    to_mate(3)
    yield
    w1, w2, acc = r["w1"], r["w2"], r["acc"]

    def first_products(kys, row):
        n = 64 * len(kys)
        for h in range(2):
            for q in range(2):
                at = q * QUART
                a = jnp.concatenate(
                    [xb[h, pl.ds(((y - ky + 4) % 4) * 4, 4), :, at : at + QUART].reshape(64, QUART) for ky in kys], axis=0
                )
                p = dot_t(a, w1[:, h * HALF + at : h * HALF + at + QUART])
                if h + q == 0:
                    acc[row : row + n] = p
                else:
                    acc[row : row + n] += p

    for ky in (0, 1, 3):
        dcp[ky].wait()
    for cp in loads:
        cp.wait()
    first_products((0, 1, 3), 0)
    yield
    for kx in (0, 1, 3, 2):
        ccp[2, kx].wait()
    to_mate(2)
    yield
    dcp[2].wait()
    first_products((2,), 192)
    first, second = acc[:, :128], acc[:, 128:]
    hidden = ((first / (1.0 + jnp.exp(-first))) * second).astype(BF).astype(F32)
    gates = jnp.concatenate(
        [xb[0, pl.ds(((y - ky + 4) % 4) * 4, 4), :, HALF:].reshape(64, 128) for ky in (0, 1, 3, 2)], axis=0
    ).astype(F32)
    col = lax.axis_index("ep")
    lane = lax.broadcasted_iota(jnp.int32, (256, 128), 1)
    g0 = jnp.sum(jnp.where(lane == col * 2, gates, 0.0), axis=1, keepdims=True)
    g1 = jnp.sum(jnp.where(lane == col * 2 + 1, gates, 0.0), axis=1, keepdims=True)
    scaled = hidden * jnp.where(lane < 64, g0, g1)
    hi = scaled.astype(BF)
    lo = (scaled - hi.astype(F32)).astype(BF)
    ybf, yown, rc = r["ybf"], r["yown"], r["rc"]
    hl = jnp.concatenate([hi, lo], axis=1)

    def second_product(h, store):
        def step(k, carry):
            at = pl.multiple_of(k * 512, 512)
            w = w2[:, pl.ds(pl.multiple_of(h * HALF + at, 128), 512)]
            out = jnp.dot(hl, jnp.concatenate([w, w], axis=0), preferred_element_type=F32)
            store(at, out.reshape(4, 4, 16, 512))
            return carry

        lax.fori_loop(0, 7, step, 0)

    def keep_bf(at, v):
        ybf[:, :, :, pl.ds(at, 512)] = v.astype(BF)

    def to_own(at, v):
        yown[:, :, :, pl.ds(at, 512)] = v

    second_product(1 - c, keep_bf)
    cps = {i: push(ybf.at[i], rc.at[i], r["se"].at[0, i], r["se"].at[1, i], mate) for i in (3, 2, 1, 0)}
    second_product(c, to_own)
    yield
    s2, r2, yacc = [r["s2a"], r["s2b"]], [r["r2a"], r["r2b"]], [r["yacca"], r["yaccb"]]

    def share(p, k, blk):
        def step(q, carry):
            at = pl.multiple_of(q * 512, 128)
            cols = pl.ds(pl.multiple_of(SPLIT[p][0] + at, 128), 512)
            if p == 0:
                v = yown[blk, :, :, cols] + rc[blk, :, :, cols].astype(F32)
            else:
                v = yown[:, blk, :, cols] + rc[:, blk, :, cols].astype(F32)
            if k == 0:
                yacc[p][:, :, pl.ds(at, 512)] = v
            else:
                s2[p][k - 1, :, :, pl.ds(at, 512)] = v.astype(BF)
            return carry

        lax.fori_loop(0, SPLIT[p][1] // 512, step, 0)

    def far_side(p, k):
        return device(x, y + k, z, c) if p == 0 else device(x + k, y, z, c)

    fcps = {}
    for k in (2, 1, 3):
        cps[PLACE[k]].wait()
        share(0, k, PLACE[k])
        fcps[0, k] = push(s2[0].at[k - 1], r2[0].at[k - 1], r["sf"].at[0, 0, k], r["sf"].at[1, 0, k], far_side(0, k))
    cps[0].wait()
    for k in (2, 1, 3):
        share(1, k, (x + k) % 4)
        fcps[1, k] = push(s2[1].at[k - 1], r2[1].at[k - 1], r["sf"].at[0, 1, k], r["sf"].at[1, 1, k], far_side(1, k))
    share(0, 0, 0)
    share(1, 0, x)
    yield
    s3, r3, zacc = [r["s3a"], r["s3b"]], [r["r3a"], r["r3b"]], [r["zacca"], r["zaccb"]]
    gcps = {}
    for p in range(2):
        for k in (1, 3, 2):
            fcps[p, k].wait()
        for k in (2, 1, 3, 0):
            b = PLACE[k] if p else (x + k) % 4
            v = yacc[p][b]
            for i in range(3):
                v = v + r2[p][i, b].astype(F32)
            if k == 0:
                zacc[p][...] = v
            else:
                s3[p][k - 1] = v.astype(BF)
                gcps[p, k] = push(s3[p].at[k - 1], r3[p].at[k - 1], r["sg"].at[0, p, k], r["sg"].at[1, p, k], far_side(1 - p, k))
    yield
    for cp in gcps.values():
        cp.wait()
    parts = []
    for p in range(2):
        v = zacc[p][...]
        for i in range(3):
            v = v + r3[p][i].astype(F32)
        parts.append(v)
    v = jnp.concatenate(parts, axis=1)
    vb = v.astype(BF)
    stack = jnp.concatenate([vb[:, j * 128 : (j + 1) * 128] for j in range(28)], axis=0)
    rows = lax.broadcasted_iota(jnp.int32, (512, 448), 0)
    cols = lax.broadcasted_iota(jnp.int32, (512, 448), 1)
    pick = jnp.where(cols == (rows % 32) * 16 + rows // 32, 1.0, 0.0).astype(BF)
    t4, r4 = r["t4"], r["r4"]
    t4[...] = jnp.dot(pick, stack, preferred_element_type=F32).astype(BF).reshape(16, 32, 128)
    cps = []
    for k in range(1, 16):
        mm = (m + k) % 16
        cps.append(push(t4.at[mm], r4.at[m], r["sh"].at[0, k], r["sh"].at[1, k], ring_member(x, y, mm)))
    r4[m] = t4[m]
    yield
    for cp in cps:
        cp.wait()
    row = []
    for h in range(2):
        tot = r4[h].astype(F32)
        for i in range(1, 8):
            tot = tot + r4[2 * i + h].astype(F32)
        row += [tot[j : j + 1] for j in range(28)]
    r["mo"][...] = jnp.concatenate(row, axis=1).astype(BF)


MOE_SCRATCH = dict(
    w1=pltpu.VMEM((256, 2 * HALF), BF),
    w2=pltpu.VMEM((128, 2 * HALF), BF),
    ra=pltpu.VMEM((16, 32, 128), BF),
    xb=pltpu.VMEM((2, 16, 16, GW), BF),
    acc=pltpu.VMEM((256, 256), F32),
    ybf=pltpu.VMEM((4, 4, 16, HALF), BF),
    yown=pltpu.VMEM((4, 4, 16, HALF), F32),
    rc=pltpu.VMEM((4, 4, 16, HALF), BF),
    s2a=pltpu.VMEM((3, 4, 16, 3072), BF),
    s2b=pltpu.VMEM((3, 4, 16, 512), BF),
    r2a=pltpu.VMEM((3, 4, 16, 3072), BF),
    r2b=pltpu.VMEM((3, 4, 16, 512), BF),
    yacca=pltpu.VMEM((4, 16, 3072), F32),
    yaccb=pltpu.VMEM((4, 16, 512), F32),
    s3a=pltpu.VMEM((3, 16, 3072), BF),
    s3b=pltpu.VMEM((3, 16, 512), BF),
    r3a=pltpu.VMEM((3, 16, 3072), BF),
    r3b=pltpu.VMEM((3, 16, 512), BF),
    zacca=pltpu.VMEM((16, 3072), F32),
    zaccb=pltpu.VMEM((16, 512), F32),
    t4=pltpu.VMEM((16, 32, 128), BF),
    r4=pltpu.VMEM((16, 32, 128), BF),
    lsem=pltpu.SemaphoreType.DMA((3,)),
    sa=pltpu.SemaphoreType.DMA((2, 16)),
    sb=pltpu.SemaphoreType.DMA((2, 4)),
    sc=pltpu.SemaphoreType.DMA((2, 4, 4)),
    sd=pltpu.SemaphoreType.DMA((2, 4)),
    se=pltpu.SemaphoreType.DMA((2, 4)),
    sf=pltpu.SemaphoreType.DMA((2, 2, 4)),
    sg=pltpu.SemaphoreType.DMA((2, 2, 4)),
    sh=pltpu.SemaphoreType.DMA((2, 16)),
)


def moe_partners():
    x, y, z, c = coords()
    m = z * 2 + c
    out = [ring_member(x, y, m + k) for k in range(1, 16)]
    out += [device(x + k, y, z, c) for k in (1, 2, 3)]
    out += [device(x, y + k, z, c) for k in (1, 2, 3)]
    return out


SCALE = 192.0 ** (-0.5)
NEG = -1e30
KV_L = 512
ORDER = (4, 3, -3, 2, -2, 1, -1, 0)


def lane_of(s):
    return s // 2, s % 2


def attn_steps(r):
    x, y, z, c = coords()
    xh, xl = x // 2, x % 2
    own = xh * 2 + c
    right, left = device(x, y, z + 1, c), device(x, y, z - 1, c)
    ahead = (right, left)

    def push(src, dst, sems, at, dev):
        cp = pltpu.make_async_remote_copy(src, dst, sems.at[(0, *at)], sems.at[(1, *at)], device_id=dev, device_id_type=MESH)
        cp.start()
        return cp

    qin, kvv, pick, mask, nl = r["q"], r["kvv"], r["pick"], r["mask"], r["nl"]
    ql, kl, ol = r["ql"], r["kl"], r["ol"]
    r["qcp"].wait()
    for i in range(2):
        ql[0, i * 160 : i * 160 + 128] = qin[i, :KV_L].astype(F32).T.astype(BF)
    rope = jnp.concatenate([qin[0, KV_L:].astype(F32), qin[1, KV_L:].astype(F32)], axis=0).T.astype(BF)
    for i in range(4):
        ql[0, 128:160, i * 128 : (i + 1) * 128] = rope[i * 32 : (i + 1) * 32]
    qcp = {}

    def send_q(d, hop):
        at = 0 if hop == 0 else 1 + d * 3 + hop - 1
        to = 1 + d * 3 + hop
        qcp[d, hop + 1] = push(ql.at[at], ql.at[to], r["sq"], (d, hop), ahead[d])

    def send_q4(d):
        at = 1 + d * 3 + 2
        rows = pl.ds(160, 128) if d else pl.ds(0, 160)
        qcp[d, 4] = push(ql.at[at, rows], ql.at[7, rows], r["sq"], (d, 3), ahead[d])

    xcp, lcp = r["xcp"], r["lcp"]

    def gather(i):
        zt = (z + ORDER[i] + 8) % 8

        def copy_page(n, carry):
            k, t = n // 2, n % 2
            to = ((xh + k // 2) % 2) * 16 + zt * 2 + (c + k) % 2
            page = kvv[pick[t, to]]
            at = pl.multiple_of(t * 32, 32)
            ol[i, k, pl.ds(at, 32)] = page[:32, :KV_L]
            ol[i, k, pl.ds(at + 64, 32)] = page[32:, :KV_L]
            rope = jnp.concatenate([page[:32, KV_L:], page[32:, KV_L:]], axis=1)
            for j in range(2):
                ol[i, k, 128:144, pl.ds(pl.multiple_of((t * 2 + j) * 128, 128), 128)] = rope[j * 16 : (j + 1) * 16]
            return carry

        lax.fori_loop(0, 8, copy_page, 0)

    r["kvcp"].wait()
    for i in range(8):
        gather(i)
    yield
    send_q(0, 0)
    send_q(1, 0)
    yield
    for hop in (1, 2, 3):
        for d in (0, 1):
            qcp[d, hop].wait()
            if hop < 3:
                send_q(d, hop)
            else:
                send_q4(d)
        yield
    lane = lax.broadcasted_iota(jnp.int32, (128, 128), 1)
    pacc, pm, ps = r["pacc"], r["pm"], r["ps"]
    ca, cs, sa, ss = r["ca"], r["cs"], r["cout"], r["csout"]

    def rope_of(at):
        return jnp.concatenate([ql[at, 128:160, j * 128 : (j + 1) * 128] for j in range(4)], axis=0)

    def partial(i, at):
        q = jnp.concatenate([ql[at, :128], ql[at, 160:]], axis=0)
        a = rope_of(at).astype(F32)
        b = pltpu.roll(a, 64, 1)
        lo = jnp.concatenate([jnp.where(lane < 64, a, 0.0), jnp.where(lane < 64, b, 0.0)], axis=0).astype(BF)
        hi = jnp.concatenate([jnp.where(lane >= 64, b, 0.0), jnp.where(lane >= 64, a, 0.0)], axis=0).astype(BF)
        kv = jnp.concatenate(
            [kl[i, n, 128:144, j * 128 : (j + 1) * 128] for n in range(4) for j in range(4)], axis=0
        )
        near, far = kl[i, :, :64].reshape(256, KV_L), kl[i, :, 64:128].reshape(256, KV_L)
        s = jnp.concatenate(
            [
                dot_t(q, near) + dot_t(lo, kv),
                dot_t(q, far) + dot_t(hi, kv),
            ],
            axis=1,
        ) * SCALE
        live = jnp.concatenate(
            [jnp.broadcast_to(mask[h, i : i + 1], (128, 512)) for h in range(2)], axis=0
        ) > 0.5
        peak = jnp.max(jnp.where(live, s, NEG), axis=1, keepdims=True)
        w = jnp.where(live, jnp.exp(s - peak), 0.0)
        pm[...] = jnp.broadcast_to(peak, (256, 128))
        ps[...] = jnp.broadcast_to(jnp.sum(w, axis=1, keepdims=True), (256, 128))
        wb = w.astype(BF)
        pacc[...] = jnp.dot(wb[:, :256], near, preferred_element_type=F32) + jnp.dot(
            wb[:, 256:], far, preferred_element_type=F32
        )

    def mine(i):
        rows = pl.ds(i * 128, 128)
        return pm[rows, 0:1], ps[rows, 0:1], pacc[rows]

    def merge(a, b):
        peak = jnp.maximum(a[0], b[0])
        u, v = jnp.exp(a[0] - peak), jnp.exp(b[0] - peak)
        return peak, a[1] * u + b[1] * v, a[2] * u + b[2] * v

    ccp = {}

    def send_part(d, dist, i, part):
        at = (d * 4 + dist - 1) * 2 + i
        sa[at] = part[2].astype(BF)
        ss[at] = jnp.where(lane == 0, part[0], part[1]).T[:8]
        ccp[d, dist, i] = [
            push(sa.at[at], ca.at[at], r["sch"], (0, at), ahead[d]),
            push(ss.at[at], cs.at[at], r["sch"], (1, at), ahead[d]),
        ]

    def came(d, dist, i):
        for cp in ccp[d, dist, i]:
            cp.wait()
        at = (d * 4 + dist - 1) * 2 + i
        st = jnp.concatenate([cs[at]] * 16, axis=0).T
        return st[:, 0:1], st[:, 1:2], ca[at].astype(F32)

    for i, dz in enumerate(ORDER):
        r["ready"](i)
        for k in (2, 3, 1):
            xcp[i, k].wait_recv()
        lcp[i].wait()
        if dz == 4:
            for d in (0, 1):
                qcp[d, 4].wait()
            partial(i, 7)
            for d in (0, 1):
                send_part(d, 4, d, mine(d))
            yield
            continue
        if dz:
            d = 0 if dz > 0 else 1
            at = 1 + (1 - d) * 3 + abs(dz) - 1
            partial(i, at)
            yield
            for part in (d, 1 - d):
                v = mine(part)
                if abs(dz) < 3 or part == d:
                    v = merge(came(d, abs(dz) + 1, part), v)
                send_part(d, abs(dz), part, v)
            yield
            continue
        partial(i, 0)
        own_rope = jnp.concatenate([nl[0:1, KV_L:], nl[1:2, KV_L:]], axis=1).astype(F32)
        for part in range(2):
            key = nl[part : part + 1].astype(F32)
            qv = ql[0, part * 160 : part * 160 + 128].astype(F32)
            rope = jnp.where(lane // 64 == part, rope_of(0).astype(F32) * own_rope, 0.0)
            score = (jnp.sum(qv * key[:, :KV_L], axis=1, keepdims=True) + jnp.sum(rope, axis=1, keepdims=True)) * SCALE
            m0, s0, a0 = mine(part)
            peak = jnp.maximum(m0, score)
            u, w = jnp.exp(m0 - peak), jnp.exp(score - peak)
            rows = pl.ds(part * 128, 128)
            pacc[rows] = a0 * u + w.astype(BF).astype(F32) * key[:, :KV_L]
            ps[rows] = jnp.broadcast_to(s0 * u + w, (128, 128))
            pm[rows] = jnp.broadcast_to(peak, (128, 128))
        yield
        for part in range(2):
            v = mine(part)
            v = merge(v, came(0, 1, part))
            v = merge(v, came(1, 1, part))
            r["ao"][part] = (v[2] / v[1]).astype(BF)


def page_steps(r):
    x, y, z, c = coords()
    own = (x // 2) * 2 + c
    ol, kl, xcp, lcp = r["ol"], r["kl"], r["xcp"], r["lcp"]

    def push(src, dst, at, dev):
        cp = pltpu.make_async_remote_copy(src, dst, r["sx"].at[(0, *at)], r["sx"].at[(1, *at)], device_id=dev, device_id_type=MESH)
        cp.start()
        return cp

    for i in range(8):
        for k in (2, 3, 1):
            to = device(x + 2 * (k // 2), y, z, c + k % 2)
            xcp[i, k] = push(ol.at[i, k], kl.at[i, own], (i, k), to)
        lcp[i] = pltpu.make_async_copy(ol.at[i, 0], kl.at[i, own], r["sl"].at[i])
        lcp[i].start()
        yield
    for cp in xcp.values():
        cp.wait_send()


ATTN_SCRATCH = dict(
    q=pltpu.VMEM((2, 576, 128), BF),
    kvv=pltpu.VMEM((32, 64, 576), BF),
    ql=pltpu.VMEM((8, 288, 512), BF),
    kl=pltpu.VMEM((8, 4, 144, 512), BF),
    ol=pltpu.VMEM((8, 4, 144, 512), BF),
    pacc=pltpu.VMEM((256, 512), F32),
    pm=pltpu.VMEM((256, 128), F32),
    ps=pltpu.VMEM((256, 128), F32),
    ca=pltpu.VMEM((16, 128, 512), BF),
    cs=pltpu.VMEM((16, 8, 128), F32),
    cout=pltpu.VMEM((16, 128, 512), BF),
    csout=pltpu.VMEM((16, 8, 128), F32),
    skv=pltpu.SemaphoreType.DMA,
    sqin=pltpu.SemaphoreType.DMA,
    sq=pltpu.SemaphoreType.DMA((2, 2, 4)),
    sx=pltpu.SemaphoreType.DMA((2, 8, 4)),
    sl=pltpu.SemaphoreType.DMA((8,)),
    sch=pltpu.SemaphoreType.DMA((2, 2, 16)),
)


def attn_partners():
    x, y, z, c = coords()
    return [
        device(x, y, z + 1, c),
        device(x, y, z - 1, c),
        device(x, y, z, 1 - c),
        device(x + 2, y, z, c),
        device(x + 2, y, z, 1 - c),
    ]


def tables_kernel(dest, req, fill, mi, ids, rw, pick, mask, tok, tf):
    g = lax.axis_index("grp")
    xh, z, c = g // 16, (g // 2) % 8, g % 2
    x = mi[...].astype(F32)
    lane = lax.broadcasted_iota(jnp.int32, (1, 128), 1)
    gates = jnp.zeros((1, 128), F32)
    for k in range(8):
        gates = gates + jnp.where(lane == ids[:, k : k + 1], rw[:, k : k + 1], 0.0)
    for h in range(2):
        for j in range(28):
            tf[h, j : j + 1] = x[:, (h * 28 + j) * 128 : (h * 28 + j + 1) * 128]
        tf[h, 28:29] = gates
        tf[h, 29:32] = jnp.zeros((3, 128), F32)
    tok[...] = tf[...].astype(BF)
    rows = lax.broadcasted_iota(jnp.int32, (128, 128), 0)
    cols = lax.broadcasted_iota(jnp.int32, (128, 128), 1)
    earlier = jnp.where((rows // 32 == cols // 32) & (cols < rows), 1.0, 0.0).astype(BF)
    code, found = [], []
    for xs in range(2):
        at = pl.multiple_of((xs * 4 + z // 2) * 128, 128)
        value = (fill[:, pl.ds(at, 128)] + 128 * req[:, pl.ds(at, 128)]).astype(F32)
        quarter = lane // 32 - (z % 2) * 2
        left = jnp.concatenate(
            [
                jnp.where(quarter == 0, value, 0.0),
                jnp.where(quarter == 1, value, 0.0),
                jnp.where(quarter == c, (lane % 32).astype(F32), 0.0),
                jnp.zeros((13, 128), F32),
            ],
            axis=0,
        ).astype(BF)
        goes = jnp.broadcast_to(dest[:, pl.ds(at, 128)].astype(F32), (128, 128)).T == cols.astype(F32)
        onehot = jnp.where(goes, 1.0, 0.0).astype(BF)
        before = jnp.dot(earlier, onehot, preferred_element_type=F32)
        at_rank = [
            jnp.dot(left, jnp.where(goes & (before == t), 1.0, 0.0).astype(BF), preferred_element_type=F32)
            for t in range(2)
        ]
        for cc in range(2):
            for t in range(2):
                code.append(at_rank[t][cc : cc + 1])
        found.append([v[2:3] for v in at_rank])
    pick[...] = jnp.concatenate(
        [jnp.where(xh == 0, found[0][t], found[1][t]).astype(jnp.int32) for t in range(2)], axis=0
    )
    codes = jnp.concatenate(code + [jnp.zeros((120, 128), F32)], axis=0).astype(BF)
    plane = lax.broadcasted_iota(jnp.int32, (16, 128), 0)
    away = jnp.zeros((16, 128), jnp.int32)
    for i, dz in enumerate(ORDER):
        away = jnp.where(plane == i, dz, away)
    target = xh * 16 + ((z + away + 8) % 8) * 2 + c
    goal = jnp.where(lax.broadcasted_iota(jnp.int32, (16, 128), 1) == target, 1.0, 0.0).astype(BF)
    slot = dot_t(goal, codes).astype(BF)
    key = lax.broadcasted_iota(jnp.int32, (128, 512), 1)
    spread = jnp.where((key // 32) % 8 == lax.broadcasted_iota(jnp.int32, (128, 512), 0), 1.0, 0.0).astype(BF)
    full = jnp.dot(slot, spread, preferred_element_type=F32)[:8]
    key = lax.broadcasted_iota(jnp.int32, (8, 512), 1)
    pos = ((key // 256) * 32 + key % 32).astype(F32)
    second = full >= 128.0
    mask[0] = jnp.where((pos < full) & ~second, 1.0, 0.0)
    mask[1] = jnp.where((pos < full - 128.0) & second, 1.0, 0.0)


SCHEDULE = "mskmkkksmmskkkkmsmmmsmsmssmsssssssmssmmss"


def merged_kernel(schedule, pick, kv, q, mask, nl, tok, wg, wu, wd, ao, mo, *scratch):
    n = len(ATTN_SCRATCH)
    ra = dict(zip(ATTN_SCRATCH, scratch[:n]), pick=pick, mask=mask, nl=nl, ao=ao)
    rm = dict(zip(MOE_SCRATCH, scratch[n:]), tok=tok, wg=wg, wu=wu, wd=wd, mo=mo)
    ra["kvcp"] = pltpu.make_async_copy(kv, ra["kvv"], ra["skv"])
    qcp = pltpu.make_async_copy(q, ra["q"], ra["sqin"])
    ra["qcp"] = qcp
    ra["kvcp"].start()
    qcp.start()
    ra["xcp"], ra["lcp"] = {}, {}
    steps = {"s": attn_steps(ra), "m": moe_steps(rm), "k": page_steps(ra)}

    def ready(i):
        while i not in ra["lcp"]:
            next(steps["k"])

    ra["ready"] = ready
    partners = moe_partners() + attn_partners()[-1:]
    greet(partners)
    next(steps["s"])
    pl.semaphore_wait(pltpu.get_barrier_semaphore(), len(partners))
    for s in schedule:
        next(steps[s], None)
    for s in "smk":
        for _ in steps[s]:
            pass


def finish_kernel(a, b, ao, bo):
    ao[...] = a[...]
    bo[...] = b[...]


def merged_call(kv_pages, page_dest, page_req, page_fill, queries, new_latent, moe_in, route_ids, route_w, w_gate, w_up, w_down):
    vm = pl.BlockSpec(memory_space=pltpu.VMEM)
    hb = pl.BlockSpec(memory_space=pl.ANY)
    pick, mask, tok = pl.pallas_call(
        tables_kernel,
        name="tables",
        out_shape=(
            jax.ShapeDtypeStruct((2, 128), jnp.int32),
            jax.ShapeDtypeStruct((2, 8, 512), F32),
            jax.ShapeDtypeStruct((2, 32, 128), BF),
        ),
        in_specs=[vm] * 6,
        out_specs=(vm, vm, vm),
        scratch_shapes=[
            pltpu.VMEM((2, 32, 128), F32),
        ],
    )(jnp.swapaxes(page_dest, 1, 2).reshape(1, -1), page_req, page_fill, moe_in, route_ids, route_w)
    shapes = (jax.ShapeDtypeStruct((2, 128, KV_L), BF), jax.ShapeDtypeStruct((1, 2 * HALF), BF))
    outs = pl.pallas_call(
        functools.partial(merged_kernel, SCHEDULE),
        name="decode",
        out_shape=shapes,
        in_specs=[pl.BlockSpec(memory_space=pltpu.SMEM), hb, hb, vm, vm, vm, hb, hb, hb],
        out_specs=(vm, vm),
        scratch_shapes=list(ATTN_SCRATCH.values()) + list(MOE_SCRATCH.values()),
        compiler_params=pltpu.CompilerParams(collective_id=0, has_side_effects=True, vmem_limit_bytes=60 * 2**20),
    )(pick, kv_pages, jnp.swapaxes(queries, 1, 2), mask, new_latent, tok, w_gate.reshape(128, -1), w_up.reshape(128, -1), w_down.reshape(128, -1))
    return pl.pallas_call(
        finish_kernel,
        name="finish",
        out_shape=shapes,
        in_specs=[vm, vm],
        out_specs=(vm, vm),
    )(*outs)


def solution(mesh):
    return jax.shard_map(
        merged_call,
        mesh=mesh,
        in_specs=(
            P(("grp", "ep"), None, None),
            P("ep", None, None),
            P("ep", None),
            P("ep", None),
            P(("grp", "ep"), None, None),
            P(("grp", "ep"), None),
            P(("grp", "ep"), None),
            P(("grp", "ep"), None),
            P(("grp", "ep"), None),
            P("ep", "grp", None),
            P("ep", "grp", None),
            P("ep", "grp", None),
        ),
        out_specs=(P(("grp", "ep"), None, None), P(("grp", "ep"), None)),
        check_vma=False,
    )
```

```python
import functools

import jax
import jax.numpy as jnp
from jax import lax
from jax.experimental import pallas as pl
from jax.experimental.pallas import tpu as pltpu
from jax.sharding import PartitionSpec as P

MESH = pl.DeviceIdType.MESH
EXPERTS = 16
HALF = 3584
QUART = 1792
SPLIT = ((0, 3072), (3072, 512))
PLACE = (0, 2, 3, 1)
GW = HALF + 128
BF = jnp.bfloat16
F32 = jnp.float32


def coords():
    g = lax.axis_index("grp")
    e = lax.axis_index("ep")
    return (g // 16) * 2 + e % 2, e // 2, (g // 2) % 8, g % 2


def device(x, y, z, c):
    x, y, z, c = (x + 4) % 4, (y + 4) % 4, (z + 8) % 8, (c + 2) % 2
    return ((x // 2) * 16 + z * 2 + c, y * 2 + x % 2)


def ring_member(x, y, m):
    m = (m + 16) % 16
    return device(x, y, m // 2, m % 2)


def greet(partners):
    sem = pltpu.get_barrier_semaphore()
    for p in partners:
        pl.semaphore_signal(sem, 1, device_id=p, device_id_type=MESH)


def dot_t(a, b):
    return lax.dot_general(a, b, (((1,), (1,)), ((), ())), preferred_element_type=F32)


def moe_steps(r):
    x, y, z, c = coords()
    m = z * 2 + c
    mate = device(x, y, z, 1 - c)

    def push(src, dst, ss, rs, dev):
        cp = pltpu.make_async_remote_copy(src, dst, ss, rs, device_id=dev, device_id_type=MESH)
        cp.start()
        return cp

    loads = [
        pltpu.make_async_copy(r["wg"], r["w1"].at[pl.ds(0, 128)], r["lsem"].at[0]),
        pltpu.make_async_copy(r["wu"], r["w1"].at[pl.ds(128, 128)], r["lsem"].at[1]),
        pltpu.make_async_copy(r["wd"], r["w2"], r["lsem"].at[2]),
    ]
    tok, ra = r["tok"], r["ra"]
    cps = []
    for k in range(1, 16):
        mm = (m + k) % 16
        cps.append(push(tok.at[mm % 2], ra.at[m], r["sa"].at[0, k], r["sa"].at[1, k], ring_member(x, y, mm)))
    for cp in loads:
        cp.start()
    ra[m] = tok[c]
    yield
    for cp in cps:
        cp.wait()
    rows = lax.broadcasted_iota(jnp.int32, (464, 512), 0)
    cols = lax.broadcasted_iota(jnp.int32, (464, 512), 1)
    pick = jnp.where(cols == (rows % 16) * 32 + rows // 16, 1.0, 0.0).astype(BF)
    got = jnp.dot(pick, ra[...].reshape(512, 128), preferred_element_type=F32).astype(BF)
    xb = r["xb"]
    mine = y * 4 + x
    for j in range(29):
        xb[c, mine, :, j * 128 : (j + 1) * 128] = got[j * 16 : (j + 1) * 16]
    up, down = device(x, y + 1, z, c), device(x, y - 1, z, c)

    def block(ky, kx):
        return ((y - ky + 4) % 4) * 4 + (x - kx + 4) % 4

    bcp, ccp, dcp = {}, {}, {}

    def to_mate(ky):
        blk = xb.at[c, pl.ds(((y - ky + 4) % 4) * 4, 4)]
        dcp[ky] = push(blk, blk, r["sd"].at[0, ky], r["sd"].at[1, ky], mate)

    def along_y(kx):
        blk = xb.at[c, block(0, kx)]
        ccp[1, kx] = push(blk, blk, r["sc"].at[0, 1, kx], r["sc"].at[1, 1, kx], up)
        ccp[3, kx] = push(blk, blk, r["sc"].at[0, 3, kx], r["sc"].at[1, 3, kx], down)

    blk = xb.at[c, mine]
    for k in (1, 3, 2):
        bcp[k] = push(blk, blk, r["sb"].at[0, k], r["sb"].at[1, k], device(x + k, y, z, c))
    along_y(0)
    yield
    for k in (1, 3):
        bcp[k].wait()
        along_y(k)
    yield
    bcp[2].wait()
    along_y(2)
    to_mate(0)
    yield
    for kx in (0, 1, 3, 2):
        for ky in (1, 3):
            ccp[ky, kx].wait()
            if (ky == 1) == (kx in (0, 2)):
                blk = xb.at[c, block(ky, kx)]
                ccp[2, kx] = push(blk, blk, r["sc"].at[0, 2, kx], r["sc"].at[1, 2, kx], up if ky == 1 else down)
        if kx in (1, 3):
            yield
    to_mate(1)
    to_mate(3)
    yield
    w1, w2, acc = r["w1"], r["w2"], r["acc"]

    def first_products(kys, row):
        n = 64 * len(kys)
        for h in range(2):
            for q in range(2):
                at = q * QUART
                a = jnp.concatenate(
                    [xb[h, pl.ds(((y - ky + 4) % 4) * 4, 4), :, at : at + QUART].reshape(64, QUART) for ky in kys], axis=0
                )
                p = dot_t(a, w1[:, h * HALF + at : h * HALF + at + QUART])
                if h + q == 0:
                    acc[row : row + n] = p
                else:
                    acc[row : row + n] += p

    for ky in (0, 1, 3):
        dcp[ky].wait()
    for cp in loads:
        cp.wait()
    first_products((0, 1, 3), 0)
    yield
    for kx in (0, 1, 3, 2):
        ccp[2, kx].wait()
    to_mate(2)
    yield
    dcp[2].wait()
    first_products((2,), 192)
    first, second = acc[:, :128], acc[:, 128:]
    hidden = ((first / (1.0 + jnp.exp(-first))) * second).astype(BF).astype(F32)
    gates = jnp.concatenate(
        [xb[0, pl.ds(((y - ky + 4) % 4) * 4, 4), :, HALF:].reshape(64, 128) for ky in (0, 1, 3, 2)], axis=0
    ).astype(F32)
    col = lax.axis_index("ep")
    lane = lax.broadcasted_iota(jnp.int32, (256, 128), 1)
    g0 = jnp.sum(jnp.where(lane == col * 2, gates, 0.0), axis=1, keepdims=True)
    g1 = jnp.sum(jnp.where(lane == col * 2 + 1, gates, 0.0), axis=1, keepdims=True)
    scaled = hidden * jnp.where(lane < 64, g0, g1)
    hi = scaled.astype(BF)
    lo = (scaled - hi.astype(F32)).astype(BF)
    ybf, yown, rc = r["ybf"], r["yown"], r["rc"]
    hl = jnp.concatenate([hi, lo], axis=1)

    def second_product(h, store):
        def step(k, carry):
            at = pl.multiple_of(k * 896, 128)
            w = w2[:, pl.ds(pl.multiple_of(h * HALF + at, 128), 896)]
            out = jnp.dot(hl, jnp.concatenate([w, w], axis=0), preferred_element_type=F32)
            store(at, out.reshape(4, 4, 16, 896))
            return carry

        lax.fori_loop(0, 4, step, 0)

    def keep_bf(at, v):
        ybf[:, :, :, pl.ds(at, 896)] = v.astype(BF)

    def to_own(at, v):
        yown[:, :, :, pl.ds(at, 896)] = v

    second_product(1 - c, keep_bf)
    cps = {i: push(ybf.at[i], rc.at[i], r["se"].at[0, i], r["se"].at[1, i], mate) for i in (3, 2, 1, 0)}
    second_product(c, to_own)
    yield
    s2, r2, yacc = [r["s2a"], r["s2b"]], [r["r2a"], r["r2b"]], [r["yacca"], r["yaccb"]]

    def share(p, k, blk):
        def step(q, carry):
            at = pl.multiple_of(q * 512, 128)
            cols = pl.ds(pl.multiple_of(SPLIT[p][0] + at, 128), 512)
            if p == 0:
                v = yown[blk, :, :, cols] + rc[blk, :, :, cols].astype(F32)
            else:
                v = yown[:, blk, :, cols] + rc[:, blk, :, cols].astype(F32)
            if k == 0:
                yacc[p][:, :, pl.ds(at, 512)] = v
            else:
                s2[p][k - 1, :, :, pl.ds(at, 512)] = v.astype(BF)
            return carry

        lax.fori_loop(0, SPLIT[p][1] // 512, step, 0)

    def far_side(p, k):
        return device(x, y + k, z, c) if p == 0 else device(x + k, y, z, c)

    fcps = {}
    for k in (2, 1, 3):
        cps[PLACE[k]].wait()
        share(0, k, PLACE[k])
        fcps[0, k] = push(s2[0].at[k - 1], r2[0].at[k - 1], r["sf"].at[0, 0, k], r["sf"].at[1, 0, k], far_side(0, k))
    cps[0].wait()
    for k in (2, 1, 3):
        share(1, k, (x + k) % 4)
        fcps[1, k] = push(s2[1].at[k - 1], r2[1].at[k - 1], r["sf"].at[0, 1, k], r["sf"].at[1, 1, k], far_side(1, k))
    share(0, 0, 0)
    share(1, 0, x)
    yield
    s3, r3, zacc = [r["s3a"], r["s3b"]], [r["r3a"], r["r3b"]], [r["zacca"], r["zaccb"]]
    gcps = {}
    for p in range(2):
        for k in (1, 3, 2):
            fcps[p, k].wait()
        for k in (2, 1, 3, 0):
            b = PLACE[k] if p else (x + k) % 4
            v = yacc[p][b]
            for i in range(3):
                v = v + r2[p][i, b].astype(F32)
            if k == 0:
                zacc[p][...] = v
            else:
                s3[p][k - 1] = v.astype(BF)
                gcps[p, k] = push(s3[p].at[k - 1], r3[p].at[k - 1], r["sg"].at[0, p, k], r["sg"].at[1, p, k], far_side(1 - p, k))
    yield
    for cp in gcps.values():
        cp.wait()
    parts = []
    for p in range(2):
        v = zacc[p][...]
        for i in range(3):
            v = v + r3[p][i].astype(F32)
        parts.append(v)
    v = jnp.concatenate(parts, axis=1)
    vb = v.astype(BF)
    stack = jnp.concatenate([vb[:, j * 128 : (j + 1) * 128] for j in range(28)], axis=0)
    rows = lax.broadcasted_iota(jnp.int32, (512, 448), 0)
    cols = lax.broadcasted_iota(jnp.int32, (512, 448), 1)
    pick = jnp.where(cols == (rows % 32) * 16 + rows // 32, 1.0, 0.0).astype(BF)
    t4, r4 = r["t4"], r["r4"]
    t4[...] = jnp.dot(pick, stack, preferred_element_type=F32).astype(BF).reshape(16, 32, 128)
    cps = []
    for k in range(1, 16):
        mm = (m + k) % 16
        cps.append(push(t4.at[mm], r4.at[m], r["sh"].at[0, k], r["sh"].at[1, k], ring_member(x, y, mm)))
    r4[m] = t4[m]
    yield
    for cp in cps:
        cp.wait()
    row = []
    for h in range(2):
        tot = r4[h].astype(F32)
        for i in range(1, 8):
            tot = tot + r4[2 * i + h].astype(F32)
        row += [tot[j : j + 1] for j in range(28)]
    r["mo"][...] = jnp.concatenate(row, axis=1).astype(BF)


MOE_SCRATCH = dict(
    w1=pltpu.VMEM((256, 2 * HALF), BF),
    w2=pltpu.VMEM((128, 2 * HALF), BF),
    ra=pltpu.VMEM((16, 32, 128), BF),
    xb=pltpu.VMEM((2, 16, 16, GW), BF),
    acc=pltpu.VMEM((256, 256), F32),
    ybf=pltpu.VMEM((4, 4, 16, HALF), BF),
    yown=pltpu.VMEM((4, 4, 16, HALF), F32),
    rc=pltpu.VMEM((4, 4, 16, HALF), BF),
    s2a=pltpu.VMEM((3, 4, 16, 3072), BF),
    s2b=pltpu.VMEM((3, 4, 16, 512), BF),
    r2a=pltpu.VMEM((3, 4, 16, 3072), BF),
    r2b=pltpu.VMEM((3, 4, 16, 512), BF),
    yacca=pltpu.VMEM((4, 16, 3072), F32),
    yaccb=pltpu.VMEM((4, 16, 512), F32),
    s3a=pltpu.VMEM((3, 16, 3072), BF),
    s3b=pltpu.VMEM((3, 16, 512), BF),
    r3a=pltpu.VMEM((3, 16, 3072), BF),
    r3b=pltpu.VMEM((3, 16, 512), BF),
    zacca=pltpu.VMEM((16, 3072), F32),
    zaccb=pltpu.VMEM((16, 512), F32),
    t4=pltpu.VMEM((16, 32, 128), BF),
    r4=pltpu.VMEM((16, 32, 128), BF),
    lsem=pltpu.SemaphoreType.DMA((3,)),
    sa=pltpu.SemaphoreType.DMA((2, 16)),
    sb=pltpu.SemaphoreType.DMA((2, 4)),
    sc=pltpu.SemaphoreType.DMA((2, 4, 4)),
    sd=pltpu.SemaphoreType.DMA((2, 4)),
    se=pltpu.SemaphoreType.DMA((2, 4)),
    sf=pltpu.SemaphoreType.DMA((2, 2, 4)),
    sg=pltpu.SemaphoreType.DMA((2, 2, 4)),
    sh=pltpu.SemaphoreType.DMA((2, 16)),
)


def moe_partners():
    x, y, z, c = coords()
    m = z * 2 + c
    out = [ring_member(x, y, m + k) for k in range(1, 16)]
    out += [device(x + k, y, z, c) for k in (1, 2, 3)]
    out += [device(x, y + k, z, c) for k in (1, 2, 3)]
    return out


SCALE = 192.0 ** (-0.5)
NEG = -1e30
KV_L = 512
ORDER = (4, 3, -3, 2, -2, 1, -1, 0)


def lane_of(s):
    return s // 2, s % 2


def attn_steps(r):
    x, y, z, c = coords()
    xh, xl = x // 2, x % 2
    own = xh * 2 + c
    right, left = device(x, y, z + 1, c), device(x, y, z - 1, c)
    ahead = (right, left)

    def push(src, dst, sems, at, dev):
        cp = pltpu.make_async_remote_copy(src, dst, sems.at[(0, *at)], sems.at[(1, *at)], device_id=dev, device_id_type=MESH)
        cp.start()
        return cp

    qin, kvv, pick, mask, nl = r["q"], r["kvv"], r["pick"], r["mask"], r["nl"]
    ql, kl, ol = r["ql"], r["kl"], r["ol"]
    r["qcp"].wait()
    for i in range(2):
        ql[0, i * 160 : i * 160 + 128] = qin[i, :KV_L].astype(F32).T.astype(BF)
    rope = jnp.concatenate([qin[0, KV_L:].astype(F32), qin[1, KV_L:].astype(F32)], axis=0).T.astype(BF)
    for i in range(4):
        ql[0, 128:160, i * 128 : (i + 1) * 128] = rope[i * 32 : (i + 1) * 32]
    qcp = {}

    def send_q(d, hop):
        at = 0 if hop == 0 else 1 + d * 3 + hop - 1
        to = 1 + d * 3 + hop
        qcp[d, hop + 1] = push(ql.at[at], ql.at[to], r["sq"], (d, hop), ahead[d])

    def send_q4(d):
        at = 1 + d * 3 + 2
        rows = pl.ds(160, 128) if d else pl.ds(0, 160)
        qcp[d, 4] = push(ql.at[at, rows], ql.at[7, rows], r["sq"], (d, 3), ahead[d])

    xcp, lcp = r["xcp"], r["lcp"]

    def gather(i):
        zt = (z + ORDER[i] + 8) % 8

        def copy_page(n, carry):
            k, t = n // 2, n % 2
            to = ((xh + k // 2) % 2) * 16 + zt * 2 + (c + k) % 2
            page = kvv[pick[t, to]]
            at = pl.multiple_of(t * 32, 32)
            ol[i, k, pl.ds(at, 32)] = page[:32, :KV_L]
            ol[i, k, pl.ds(at + 64, 32)] = page[32:, :KV_L]
            rope = jnp.concatenate([page[:32, KV_L:], page[32:, KV_L:]], axis=1)
            for j in range(2):
                ol[i, k, 128:144, pl.ds(pl.multiple_of((t * 2 + j) * 128, 128), 128)] = rope[j * 16 : (j + 1) * 16]
            return carry

        lax.fori_loop(0, 8, copy_page, 0)

    r["kvcp"].wait()
    for i in range(8):
        gather(i)
    yield
    send_q(0, 0)
    send_q(1, 0)
    yield
    for hop in (1, 2, 3):
        for d in (0, 1):
            qcp[d, hop].wait()
            if hop < 3:
                send_q(d, hop)
            else:
                send_q4(d)
        yield
    lane = lax.broadcasted_iota(jnp.int32, (128, 128), 1)
    pacc, pm, ps = r["pacc"], r["pm"], r["ps"]
    ca, cs, sa, ss = r["ca"], r["cs"], r["cout"], r["csout"]

    def rope_of(at):
        return jnp.concatenate([ql[at, 128:160, j * 128 : (j + 1) * 128] for j in range(4)], axis=0)

    def partial(i, at):
        q = jnp.concatenate([ql[at, :128], ql[at, 160:]], axis=0)
        a = rope_of(at).astype(F32)
        b = pltpu.roll(a, 64, 1)
        lo = jnp.concatenate([jnp.where(lane < 64, a, 0.0), jnp.where(lane < 64, b, 0.0)], axis=0).astype(BF)
        hi = jnp.concatenate([jnp.where(lane >= 64, b, 0.0), jnp.where(lane >= 64, a, 0.0)], axis=0).astype(BF)
        kv = jnp.concatenate(
            [kl[i, n, 128:144, j * 128 : (j + 1) * 128] for n in range(4) for j in range(4)], axis=0
        )
        near, far = kl[i, :, :64].reshape(256, KV_L), kl[i, :, 64:128].reshape(256, KV_L)
        s = jnp.concatenate(
            [
                dot_t(q, near) + dot_t(lo, kv),
                dot_t(q, far) + dot_t(hi, kv),
            ],
            axis=1,
        ) * SCALE
        live = jnp.concatenate(
            [jnp.broadcast_to(mask[h, i : i + 1], (128, 512)) for h in range(2)], axis=0
        ) > 0.5
        peak = jnp.max(jnp.where(live, s, NEG), axis=1, keepdims=True)
        w = jnp.where(live, jnp.exp(s - peak), 0.0)
        pm[...] = jnp.broadcast_to(peak, (256, 128))
        ps[...] = jnp.broadcast_to(jnp.sum(w, axis=1, keepdims=True), (256, 128))
        wb = w.astype(BF)
        pacc[...] = jnp.dot(wb[:, :256], near, preferred_element_type=F32) + jnp.dot(
            wb[:, 256:], far, preferred_element_type=F32
        )

    def mine(i):
        rows = pl.ds(i * 128, 128)
        return pm[rows, 0:1], ps[rows, 0:1], pacc[rows]

    def merge(a, b):
        peak = jnp.maximum(a[0], b[0])
        u, v = jnp.exp(a[0] - peak), jnp.exp(b[0] - peak)
        return peak, a[1] * u + b[1] * v, a[2] * u + b[2] * v

    ccp = {}

    def send_part(d, dist, i, part):
        at = (d * 4 + dist - 1) * 2 + i
        sa[at] = part[2].astype(BF)
        ss[at] = jnp.where(lane == 0, part[0], part[1]).T[:8]
        ccp[d, dist, i] = [
            push(sa.at[at], ca.at[at], r["sch"], (0, at), ahead[d]),
            push(ss.at[at], cs.at[at], r["sch"], (1, at), ahead[d]),
        ]

    def came(d, dist, i):
        for cp in ccp[d, dist, i]:
            cp.wait()
        at = (d * 4 + dist - 1) * 2 + i
        st = jnp.concatenate([cs[at]] * 16, axis=0).T
        return st[:, 0:1], st[:, 1:2], ca[at].astype(F32)

    for i, dz in enumerate(ORDER):
        r["ready"](i)
        for k in (2, 3, 1):
            xcp[i, k].wait_recv()
        lcp[i].wait()
        if dz == 4:
            for d in (0, 1):
                qcp[d, 4].wait()
            partial(i, 7)
            for d in (0, 1):
                send_part(d, 4, d, mine(d))
            yield
            continue
        if dz:
            d = 0 if dz > 0 else 1
            at = 1 + (1 - d) * 3 + abs(dz) - 1
            partial(i, at)
            yield
            for part in (d, 1 - d):
                v = mine(part)
                if abs(dz) < 3 or part == d:
                    v = merge(came(d, abs(dz) + 1, part), v)
                send_part(d, abs(dz), part, v)
            yield
            continue
        partial(i, 0)
        own_rope = jnp.concatenate([nl[0:1, KV_L:], nl[1:2, KV_L:]], axis=1).astype(F32)
        for part in range(2):
            key = nl[part : part + 1].astype(F32)
            qv = ql[0, part * 160 : part * 160 + 128].astype(F32)
            rope = jnp.where(lane // 64 == part, rope_of(0).astype(F32) * own_rope, 0.0)
            score = (jnp.sum(qv * key[:, :KV_L], axis=1, keepdims=True) + jnp.sum(rope, axis=1, keepdims=True)) * SCALE
            m0, s0, a0 = mine(part)
            peak = jnp.maximum(m0, score)
            u, w = jnp.exp(m0 - peak), jnp.exp(score - peak)
            rows = pl.ds(part * 128, 128)
            pacc[rows] = a0 * u + w.astype(BF).astype(F32) * key[:, :KV_L]
            ps[rows] = jnp.broadcast_to(s0 * u + w, (128, 128))
            pm[rows] = jnp.broadcast_to(peak, (128, 128))
        yield
        for part in range(2):
            v = mine(part)
            v = merge(v, came(0, 1, part))
            v = merge(v, came(1, 1, part))
            r["ao"][part] = (v[2] / v[1]).astype(BF)


def page_steps(r):
    x, y, z, c = coords()
    own = (x // 2) * 2 + c
    ol, kl, xcp, lcp = r["ol"], r["kl"], r["xcp"], r["lcp"]

    def push(src, dst, at, dev):
        cp = pltpu.make_async_remote_copy(src, dst, r["sx"].at[(0, *at)], r["sx"].at[(1, *at)], device_id=dev, device_id_type=MESH)
        cp.start()
        return cp

    for i in range(8):
        for k in (2, 3, 1):
            to = device(x + 2 * (k // 2), y, z, c + k % 2)
            xcp[i, k] = push(ol.at[i, k], kl.at[i, own], (i, k), to)
        lcp[i] = pltpu.make_async_copy(ol.at[i, 0], kl.at[i, own], r["sl"].at[i])
        lcp[i].start()
        yield
    for cp in xcp.values():
        cp.wait_send()


ATTN_SCRATCH = dict(
    q=pltpu.VMEM((2, 576, 128), BF),
    kvv=pltpu.VMEM((32, 64, 576), BF),
    ql=pltpu.VMEM((8, 288, 512), BF),
    kl=pltpu.VMEM((8, 4, 144, 512), BF),
    ol=pltpu.VMEM((8, 4, 144, 512), BF),
    pacc=pltpu.VMEM((256, 512), F32),
    pm=pltpu.VMEM((256, 128), F32),
    ps=pltpu.VMEM((256, 128), F32),
    ca=pltpu.VMEM((16, 128, 512), BF),
    cs=pltpu.VMEM((16, 8, 128), F32),
    cout=pltpu.VMEM((16, 128, 512), BF),
    csout=pltpu.VMEM((16, 8, 128), F32),
    skv=pltpu.SemaphoreType.DMA,
    sqin=pltpu.SemaphoreType.DMA,
    sq=pltpu.SemaphoreType.DMA((2, 2, 4)),
    sx=pltpu.SemaphoreType.DMA((2, 8, 4)),
    sl=pltpu.SemaphoreType.DMA((8,)),
    sch=pltpu.SemaphoreType.DMA((2, 2, 16)),
)


def attn_partners():
    x, y, z, c = coords()
    return [
        device(x, y, z + 1, c),
        device(x, y, z - 1, c),
        device(x, y, z, 1 - c),
        device(x + 2, y, z, c),
        device(x + 2, y, z, 1 - c),
    ]


def tables_kernel(dest, req, fill, mi, ids, rw, pick, mask, tok, tf):
    g = lax.axis_index("grp")
    xh, z, c = g // 16, (g // 2) % 8, g % 2
    x = mi[...].astype(F32)
    lane = lax.broadcasted_iota(jnp.int32, (1, 128), 1)
    gates = jnp.zeros((1, 128), F32)
    for k in range(8):
        gates = gates + jnp.where(lane == ids[:, k : k + 1], rw[:, k : k + 1], 0.0)
    for h in range(2):
        for j in range(28):
            tf[h, j : j + 1] = x[:, (h * 28 + j) * 128 : (h * 28 + j + 1) * 128]
        tf[h, 28:29] = gates
        tf[h, 29:32] = jnp.zeros((3, 128), F32)
    tok[...] = tf[...].astype(BF)
    rows = lax.broadcasted_iota(jnp.int32, (128, 128), 0)
    cols = lax.broadcasted_iota(jnp.int32, (128, 128), 1)
    earlier = jnp.where((rows // 32 == cols // 32) & (cols < rows), 1.0, 0.0).astype(BF)
    code, found = [], []
    for xs in range(2):
        at = pl.multiple_of((xs * 4 + z // 2) * 128, 128)
        value = (fill[:, pl.ds(at, 128)] + 128 * req[:, pl.ds(at, 128)]).astype(F32)
        quarter = lane // 32 - (z % 2) * 2
        left = jnp.concatenate(
            [
                jnp.where(quarter == 0, value, 0.0),
                jnp.where(quarter == 1, value, 0.0),
                jnp.where(quarter == c, (lane % 32).astype(F32), 0.0),
                jnp.zeros((13, 128), F32),
            ],
            axis=0,
        ).astype(BF)
        goes = jnp.broadcast_to(dest[:, pl.ds(at, 128)].astype(F32), (128, 128)).T == cols.astype(F32)
        onehot = jnp.where(goes, 1.0, 0.0).astype(BF)
        before = jnp.dot(earlier, onehot, preferred_element_type=F32)
        at_rank = [
            jnp.dot(left, jnp.where(goes & (before == t), 1.0, 0.0).astype(BF), preferred_element_type=F32)
            for t in range(2)
        ]
        for cc in range(2):
            for t in range(2):
                code.append(at_rank[t][cc : cc + 1])
        found.append([v[2:3] for v in at_rank])
    pick[...] = jnp.concatenate(
        [jnp.where(xh == 0, found[0][t], found[1][t]).astype(jnp.int32) for t in range(2)], axis=0
    )
    codes = jnp.concatenate(code + [jnp.zeros((120, 128), F32)], axis=0).astype(BF)
    plane = lax.broadcasted_iota(jnp.int32, (16, 128), 0)
    away = jnp.zeros((16, 128), jnp.int32)
    for i, dz in enumerate(ORDER):
        away = jnp.where(plane == i, dz, away)
    target = xh * 16 + ((z + away + 8) % 8) * 2 + c
    goal = jnp.where(lax.broadcasted_iota(jnp.int32, (16, 128), 1) == target, 1.0, 0.0).astype(BF)
    slot = dot_t(goal, codes).astype(BF)
    key = lax.broadcasted_iota(jnp.int32, (128, 512), 1)
    spread = jnp.where((key // 32) % 8 == lax.broadcasted_iota(jnp.int32, (128, 512), 0), 1.0, 0.0).astype(BF)
    full = jnp.dot(slot, spread, preferred_element_type=F32)[:8]
    key = lax.broadcasted_iota(jnp.int32, (8, 512), 1)
    pos = ((key // 256) * 32 + key % 32).astype(F32)
    second = full >= 128.0
    mask[0] = jnp.where((pos < full) & ~second, 1.0, 0.0)
    mask[1] = jnp.where((pos < full - 128.0) & second, 1.0, 0.0)


SCHEDULE = "mskmkkksmmskkkkmsmmmsmsmssmsssssssmssmmss"


def merged_kernel(schedule, pick, kv, q, mask, nl, tok, wg, wu, wd, ao, mo, *scratch):
    n = len(ATTN_SCRATCH)
    ra = dict(zip(ATTN_SCRATCH, scratch[:n]), pick=pick, mask=mask, nl=nl, ao=ao)
    rm = dict(zip(MOE_SCRATCH, scratch[n:]), tok=tok, wg=wg, wu=wu, wd=wd, mo=mo)
    ra["kvcp"] = pltpu.make_async_copy(kv, ra["kvv"], ra["skv"])
    qcp = pltpu.make_async_copy(q, ra["q"], ra["sqin"])
    ra["qcp"] = qcp
    ra["kvcp"].start()
    qcp.start()
    ra["xcp"], ra["lcp"] = {}, {}
    steps = {"s": attn_steps(ra), "m": moe_steps(rm), "k": page_steps(ra)}

    def ready(i):
        while i not in ra["lcp"]:
            next(steps["k"])

    ra["ready"] = ready
    partners = moe_partners() + attn_partners()[-1:]
    greet(partners)
    next(steps["s"])
    pl.semaphore_wait(pltpu.get_barrier_semaphore(), len(partners))
    for s in schedule:
        next(steps[s], None)
    for s in "smk":
        for _ in steps[s]:
            pass


def finish_kernel(a, b, ao, bo):
    ao[...] = a[...]
    bo[...] = b[...]


def merged_call(kv_pages, page_dest, page_req, page_fill, queries, new_latent, moe_in, route_ids, route_w, w_gate, w_up, w_down):
    vm = pl.BlockSpec(memory_space=pltpu.VMEM)
    hb = pl.BlockSpec(memory_space=pl.ANY)
    pick, mask, tok = pl.pallas_call(
        tables_kernel,
        name="tables",
        out_shape=(
            jax.ShapeDtypeStruct((2, 128), jnp.int32),
            jax.ShapeDtypeStruct((2, 8, 512), F32),
            jax.ShapeDtypeStruct((2, 32, 128), BF),
        ),
        in_specs=[vm] * 6,
        out_specs=(vm, vm, vm),
        scratch_shapes=[
            pltpu.VMEM((2, 32, 128), F32),
        ],
    )(jnp.swapaxes(page_dest, 1, 2).reshape(1, -1), page_req, page_fill, moe_in, route_ids, route_w)
    shapes = (jax.ShapeDtypeStruct((2, 128, KV_L), BF), jax.ShapeDtypeStruct((1, 2 * HALF), BF))
    outs = pl.pallas_call(
        functools.partial(merged_kernel, SCHEDULE),
        name="decode",
        out_shape=shapes,
        in_specs=[pl.BlockSpec(memory_space=pltpu.SMEM), hb, hb, vm, vm, vm, hb, hb, hb],
        out_specs=(vm, vm),
        scratch_shapes=list(ATTN_SCRATCH.values()) + list(MOE_SCRATCH.values()),
        compiler_params=pltpu.CompilerParams(collective_id=0, has_side_effects=True, vmem_limit_bytes=60 * 2**20),
    )(pick, kv_pages, jnp.swapaxes(queries, 1, 2), mask, new_latent, tok, w_gate.reshape(128, -1), w_up.reshape(128, -1), w_down.reshape(128, -1))
    return pl.pallas_call(
        finish_kernel,
        name="finish",
        out_shape=shapes,
        in_specs=[vm, vm],
        out_specs=(vm, vm),
    )(*outs)


def solution(mesh):
    return jax.shard_map(
        merged_call,
        mesh=mesh,
        in_specs=(
            P(("grp", "ep"), None, None),
            P("ep", None, None),
            P("ep", None),
            P("ep", None),
            P(("grp", "ep"), None, None),
            P(("grp", "ep"), None),
            P(("grp", "ep"), None),
            P(("grp", "ep"), None),
            P(("grp", "ep"), None),
            P("ep", "grp", None),
            P("ep", "grp", None),
            P("ep", "grp", None),
        ),
        out_specs=(P(("grp", "ep"), None, None), P(("grp", "ep"), None)),
        check_vma=False,
    )
```
